128 devices in a mesh: section: 4 (over x), dp: 32 (over y, z, core).
Axes of the slice: x: 4, y: 4, z: 4, core: 2. Of those that a mesh axis runs over, the one named last changes fastest.
Arguments:
- patches: bfloat16 [2, 32, 128, 1024], P(None, 'dp'), may hold values from -6 to 6
- segment_ids: int32 [2, 32, 128], P(None, 'dp'), may hold values from 0 to 3, never falling along the last dimension, each value on 1 to 64 neighbouring positions
- weights_qkv: bfloat16 [4, 1024, 3072], P('section'), may hold values from -0.1875 to 0.1875
- weights_out: bfloat16 [4, 1024, 1024], P('section'), may hold values from -0.375 to 0.375
- cotangent: bfloat16 [2, 32, 128, 1024], P(None, 'dp'), may hold values from -6 to 6
Outputs:
- section_outputs: bfloat16 [4, 2, 32, 128, 1024], P('section', None, 'dp')
- section_input_grads: bfloat16 [4, 2, 32, 128, 1024], P('section', None, 'dp')
- grad_qkv: float32 [4, 1024, 3072], P('section', 'dp')
- grad_out: float32 [4, 1024, 1024], P('section', None, 'dp')
The draws below stay inside these ranges and needn't reach their ends.
Inputs may be any that keep to these rules, and one draw needn't show every extreme that they name: `segment_ids`: within each packed sequence the ids never fall; each image holds 1 to 64 patches, one exactly that many.
All inputs are finite; a program needn't handle non-finite values.
Results may differ from the reference program's by a relative error of at most 0.03.
Values may be sent and summed in bfloat16 or wider, within the bound.
A program may use at most 128 MiB of HBM per device.

```python
import math
import jax
import jax.numpy as jnp
import numpy as np
from jax import lax

D = 1024
HEAD_DIM = 64
INNER = 1024
SEQ = 128
MICRO = 2
IMGS = 4
SECTIONS = 4
PACKS = 32


def level_of(key, extent, pieces, smallest, largest):
    factor_of = 1.0
    for position, blocks in pieces:
        steps = jax.random.uniform(jax.random.fold_in(jax.random.fold_in(key, 6), position), (blocks,), jnp.float32, smallest / len(pieces), largest / len(pieces))
        factor_of = factor_of * jnp.repeat(jnp.exp(steps), extent[position] // blocks).reshape((-1,) + (1,) * (len(extent) - 1 - position))
    return factor_of


def length_profile(amount, total, most, skew):
    weights = [(1 << 20) // math.isqrt(standing ** skew) + 1 for standing in range(2, amount + 1)]
    surplus, holding = total - most - (amount - 1), [1] * (amount - 1)
    while surplus > 0:
        movable = [i for i in range(amount - 1) if holding[i] < most]
        pool, left = sum([weights[i] for i in movable]), surplus
        for i in movable:
            addition = min(most - holding[i], max(1, left * weights[i] // pool), surplus)
            holding[i] = holding[i] + addition
            surplus = surplus - addition
    return np.array([most] + holding)


def uneven(rng, count, total, reach, lean):
    if count == 2:
        one = jax.random.randint(rng, (), max(1, total - reach), min(reach, total - 1) + 1)
        return jnp.stack([one, total - one])
    tallies = jnp.asarray(length_profile(count, total, reach, lean), jnp.int32)
    pairs = (count - 1) // 2
    giver, receiver = tallies[1:1 + 2 * pairs:2], tallies[2:2 + 2 * pairs:2]
    room = jnp.minimum(giver - 1, reach - receiver)
    passed = jax.random.randint(jax.random.fold_in(rng, 1), (pairs,), 0, 1 << 20) % (room + 1)
    tallies = tallies.at[1:1 + 2 * pairs:2].set(giver - passed).at[2:2 + 2 * pairs:2].set(receiver + passed)
    return tallies[jax.random.permutation(jax.random.fold_in(rng, 2), count)]


def gaussian(own_key, shape, deviation, limit, cuts=(), held_as=jnp.bfloat16):
    result = deviation * jax.random.normal(own_key, shape, jnp.float32)
    if cuts:
        result = result * level_of(own_key, shape, cuts, -0.22, 0.18)
    return jnp.clip(result, -limit, limit).astype(held_as)


def setup_inputs(seed: int = 0) -> dict:
    key_of = jax.random.split(jax.random.key(seed), 6)
    return {
        "patches": gaussian(key_of[0], (MICRO, PACKS, SEQ, D), 1.0, 6.0, ((1, 32),)),
        "segment_ids": jax.vmap(lambda own: jnp.searchsorted(jnp.cumsum(uneven(own, IMGS, SEQ, SEQ // 2, 2)), jnp.arange(SEQ), side="right"))(jax.random.split(key_of[1], MICRO * PACKS)).reshape((MICRO, PACKS, SEQ)).astype(jnp.int32),
        "weights_qkv": gaussian(key_of[2], (SECTIONS, D, 3 * INNER), D ** -0.5, 0.1875, ((0, 4),)),
        "weights_out": gaussian(key_of[3], (SECTIONS, INNER, D), (INNER // 4) ** -0.5, 0.375, ((0, 4),)),
        "cotangent": gaussian(key_of[4], (MICRO, PACKS, SEQ, D), 1.0, 6.0, ((1, 32),)),
    }


epsilon = 1e-06

def layer_norm(values):
    average = lax.optimization_barrier(jnp.mean(values, axis=-1, keepdims=True))
    centred = values - average
    variance = lax.optimization_barrier(jnp.mean(centred * centred, axis=-1, keepdims=True))
    return centred * lax.rsqrt(variance + epsilon)

def attend(projected, segments):
    packs, length = segments.shape
    inner = projected.shape[-1] // 3
    queries = layer_norm(projected[..., :inner].reshape(packs, length, -1, HEAD_DIM))
    key_rows = layer_norm(projected[..., inner:2 * inner].reshape(packs, length, -1, HEAD_DIM))
    value_rows = projected[..., 2 * inner:].astype(jnp.bfloat16).reshape(packs, length, -1, HEAD_DIM)
    scores = jnp.einsum('pshd,pthd->phst', queries, key_rows) / math.sqrt(HEAD_DIM)
    allowed = (segments[:, :, None] == segments[:, None, :])[:, None, :, :]
    weights = jnp.where(allowed, jnp.exp(scores), 0.0)
    probs = (weights / lax.optimization_barrier(jnp.sum(weights, axis=-1, keepdims=True))).astype(jnp.bfloat16)
    mixed = jnp.einsum('phst,pthd->pshd', probs.astype(jnp.float32), value_rows.astype(jnp.float32))
    return mixed.reshape(packs, length, inner)

def forward(inputs, segments, w_qkv, w_out):
    packs, length, width = inputs.shape
    widened = inputs.astype(jnp.float32)
    normed = layer_norm(widened).astype(jnp.bfloat16)
    projected = jnp.dot(normed.reshape(-1, width), w_qkv, preferred_element_type=jnp.float32).reshape(packs, length, -1)
    mixed = attend(projected, segments).astype(jnp.bfloat16)
    branch = jnp.dot(mixed.reshape(-1, mixed.shape[-1]), w_out, preferred_element_type=jnp.float32).reshape(packs, length, width)
    return ((widened + branch).astype(jnp.bfloat16), normed, projected, mixed)

def backward(inputs, segments, w_qkv, w_out, upstream):
    packs, length, width = inputs.shape
    unused, normed, projected, mixed = forward(inputs, segments, w_qkv, w_out)
    inner = mixed.shape[-1]
    rows = upstream.reshape(-1, width)
    grad_out = lax.dot_general(mixed.reshape(-1, inner), rows, (((0,), (0,)), ((), ())), preferred_element_type=jnp.float32)
    grad_mixed = lax.dot_general(rows, w_out, (((1,), (1,)), ((), ())), preferred_element_type=jnp.float32)
    grad_mixed = grad_mixed.astype(jnp.bfloat16).reshape(packs, length, inner)
    unused_attend, pull_attend = jax.vjp(lambda values: attend(values, segments), projected)
    grad_projected = pull_attend(grad_mixed.astype(jnp.float32))[0].astype(jnp.bfloat16).reshape(-1, 3 * inner)
    grad_qkv = lax.dot_general(normed.reshape(-1, width), grad_projected, (((0,), (0,)), ((), ())), preferred_element_type=jnp.float32)
    grad_normed = lax.dot_general(grad_projected, w_qkv, (((1,), (1,)), ((), ())), preferred_element_type=jnp.float32)
    unused_norm, pull_norm = jax.vjp(layer_norm, inputs.astype(jnp.float32))
    grad_inputs = upstream.astype(jnp.float32) + pull_norm(grad_normed.reshape(packs, length, width))[0]
    return (grad_inputs.astype(jnp.bfloat16), grad_qkv, grad_out)

def reference(patches, segment_ids, weights_qkv, weights_out, cotangent):
    entries = [[None] * MICRO for section in range(SECTIONS)]
    results = [[None] * MICRO for section in range(SECTIONS)]
    for micro in range(MICRO):
        current = patches[micro]
        for section in range(SECTIONS):
            entries[section][micro] = current
            current = forward(current, segment_ids[micro], weights_qkv[section], weights_out[section])[0]
            results[section][micro] = current
    grads_in = [[None] * MICRO for section in range(SECTIONS)]
    totals_qkv = [jnp.zeros(weights_qkv.shape[1:], jnp.float32) for section in range(SECTIONS)]
    totals_out = [jnp.zeros(weights_out.shape[1:], jnp.float32) for section in range(SECTIONS)]
    for micro in range(MICRO):
        upstream = cotangent[micro]
        for section in reversed(range(SECTIONS)):
            upstream, part_qkv, part_out = backward(entries[section][micro], segment_ids[micro], weights_qkv[section], weights_out[section], upstream)
            grads_in[section][micro] = upstream
            totals_qkv[section] = totals_qkv[section] + part_qkv
            totals_out[section] = totals_out[section] + part_out
    section_outputs = jnp.stack([jnp.stack(row) for row in results])
    section_input_grads = jnp.stack([jnp.stack(row) for row in grads_in])
    return (section_outputs, section_input_grads, jnp.stack(totals_qkv), jnp.stack(totals_out))
```

```python
import functools

import jax
import jax.numpy as jnp
from jax import lax
from jax.experimental import pallas as pl
from jax.experimental.pallas import tpu as pltpu
from jax.sharding import PartitionSpec as P

BF16 = jnp.bfloat16
F32 = jnp.float32
EPSILON = 1e-6
MESH = pl.DeviceIdType.MESH


def dg(a,b,ca=1,cb=0): return lax.dot_general(a,b,(((ca,),(cb,)),((),())),preferred_element_type=F32)

def block_diagonal(pair):
    blank = jnp.zeros((64, pair.shape[1]), pair.dtype)
    top = jnp.concatenate([pair[:64], blank], axis=1)
    bottom = jnp.concatenate([blank, pair[64:]], axis=1)
    return jnp.concatenate([top, bottom], axis=0)

def head_norm(rows):
    grouped = rows.reshape(2, 64, rows.shape[1])
    centred = grouped - jnp.mean(grouped, axis=1, keepdims=True)
    inverse = lax.rsqrt(jnp.mean(centred * centred, axis=1, keepdims=True) + EPSILON)
    return (centred * inverse).reshape(rows.shape), inverse[:, 0, :]

def head_norm_pull(grad, normed, inverse):
    tokens = grad.shape[1]
    g = grad.reshape(2, 64, tokens)
    n = normed.reshape(2, 64, tokens)
    first = jnp.mean(g, axis=1, keepdims=True)
    second = jnp.mean(g * n, axis=1, keepdims=True)
    return ((g - first - n * second) * inverse[:, None, :]).reshape(grad.shape)

def forward_step(m, r):
    x = r["xin"][m].astype(F32)
    centred = x - jnp.mean(x, axis=-1, keepdims=True)
    inverse = lax.rsqrt(jnp.mean(centred * centred, axis=-1, keepdims=True) + EPSILON)
    r["xinv"][m] = jnp.broadcast_to(inverse, (128, 128))
    r["normed"][m] = (centred * inverse).astype(BF16)
    queries_in = jnp.broadcast_to(r["segments"][m].astype(F32), (128, 128))
    allowed = queries_in == queries_in.T
    allowed = jnp.concatenate([allowed, allowed], axis=1)
    for quad in range(4):
        normed = r["normed"][m]
        q4 = dg(normed, r["wqkv"][:, 256*quad:256*quad+256])
        k4 = dg(normed, r["wqkv"][:, 1024+256*quad:1024+256*quad+256])
        v4 = dg(normed, r["wqkv"][:, 2048+256*quad:2048+256*quad+256]).astype(BF16)
        for half in range(2):
            pair = 2*quad+half
            c = slice(128*half, 128*half+128)
            q, qi = head_norm(q4[:, c].T)
            k, ki = head_norm(k4[:, c].T)
            qs = (q * 0.125).astype(BF16)
            kt = k.astype(BF16)
            v = v4[:, c]
            r["qs"][m, pair] = qs
            r["kt"][m, pair] = kt
            r["v"][m, pair] = v
            r["qi"][m, pair] = qi
            r["ki"][m, pair] = ki
            scores = dg(kt.T, block_diagonal(qs))
            w = jnp.where(allowed, jnp.exp(scores), 0.0)
            p = (w * (1.0 / jnp.sum(w, axis=0, keepdims=True))).astype(BF16)
            r["probs"][m, pair] = p
            vt = v.T
            o = jnp.concatenate([dg(vt[:64], p[:, :128]), dg(vt[64:], p[:, 128:])], axis=0).astype(BF16)
            r["mixed"][m, :, 128*pair:128*pair+128] = o.T
    mixed = r["mixed"][m]
    for j in range(4):
        c = slice(256*j, 256*j+256)
        branch = dg(mixed, r["wout"][:, c])
        r["xout"][m, :, c] = (r["xin"][m, :, c].astype(F32) + branch).astype(BF16)

def backward_step(m, r):
    g = r["gin"][m]
    for quad in range(4):
        go4 = dg(g, r["wout_t"][:, 256*quad:256*quad+256]).astype(BF16)
        for half in range(2):
            pair = 2*quad+half
            go = go4[:, 128*half:128*half+128]
            got = go.T
            p = r["probs"][m, pair]
            dp = dg(r["v"][m, pair], block_diagonal(got))
            pd = p.astype(F32) * dp
            ds = (pd - p.astype(F32) * jnp.sum(pd, axis=0, keepdims=True)).astype(BF16)
            kt = r["kt"][m, pair]; qs = r["qs"][m, pair]
            gq = jnp.concatenate([dg(kt[:64], ds[:, :128]), dg(kt[64:], ds[:, 128:])], axis=0)
            gk = jnp.concatenate([dg(qs[:64], ds[:, :128], 1, 1), dg(qs[64:], ds[:, 128:], 1, 1)], axis=0)
            gv = jnp.concatenate([dg(got[:64], p[:, :128], 1, 1), dg(got[64:], p[:, 128:], 1, 1)], axis=0).astype(BF16).T
            gq = head_norm_pull(gq * 0.125, qs.astype(F32) * 8.0, r["qi"][m, pair])
            gk = head_norm_pull(gk, kt.astype(F32), r["ki"][m, pair])
            r["gproj"][m, :, 128*pair:128*pair+128] = gq.astype(BF16).T
            r["gproj"][m, :, 1024+128*pair:1024+128*pair+128] = gk.astype(BF16).T
            r["gproj"][m, :, 2048+128*pair:2048+128*pair+128] = gv
    gproj = r["gproj"][m]
    for j in range(4):
        r["gn"][:, 256*j:256*j+256] = dg(gproj, r["wqkv_t"][:, 256*j:256*j+256])
    gn = r["gn"][...]
    n = r["normed"][m].astype(F32)
    first = jnp.mean(gn, axis=-1, keepdims=True)
    second = jnp.mean(gn * n, axis=-1, keepdims=True)
    dx = (gn - first - n * second) * r["xinv"][m][:, :1]
    r["gout"][m] = (r["gin"][m].astype(F32) + dx).astype(BF16)

def transpose_weights(r):
    for j in range(8):
        r["wqkv_t"][:, 128*j:128*j+128] = r["wqkv"][128*j:128*j+128, :].T
        r["wout_t"][:, 128*j:128*j+128] = r["wout"][128*j:128*j+128, :].T


def relay_kernel(names, *refs):
    r = dict(zip(names, refs))
    section = lax.axis_index("section")
    last = lax.axis_size("section") - 1
    after = lax.rem(section + 1, last + 1)
    before = lax.rem(section + last, last + 1)
    is_first = section == 0
    is_last = section == last

    loads = [
        pltpu.make_async_copy(r["w_qkv_hbm"].at[0], r["wqkv"], r["load"].at[0]),
        pltpu.make_async_copy(r["w_out_hbm"].at[0], r["wout"], r["load"].at[1]),
    ]

    def entry(m):
        return pltpu.make_async_copy(r["patches"].at[m, 0], r["xin"].at[m], r["load"].at[2 + m])

    def end_gradient(m):
        return pltpu.make_async_copy(r["cotangent"].at[m, 0], r["gin"].at[m], r["load"].at[4 + m])

    def pass_on(m):
        return pltpu.make_async_remote_copy(
            src_ref=r["xout"].at[m], dst_ref=r["xin"].at[m],
            send_sem=r["x_send"].at[m], recv_sem=r["x_recv"].at[m],
            device_id={"section": after}, device_id_type=MESH,
        )

    def pass_back(m):
        return pltpu.make_async_remote_copy(
            src_ref=r["gout"].at[m], dst_ref=r["gin"].at[m],
            send_sem=r["g_send"].at[m], recv_sem=r["g_recv"].at[m],
            device_id={"section": before}, device_id_type=MESH,
        )

    def keep_output(m):
        return pltpu.make_async_copy(r["xout"].at[m], r["outputs"].at[0, m, 0], r["store"].at[m])

    def keep_gradient(m):
        return pltpu.make_async_copy(r["gout"].at[m], r["input_grads"].at[0, m, 0], r["store"].at[2 + m])

    @pl.when(is_first)
    def _():
        for m in range(2):
            entry(m).start()

    for load in loads:
        load.start()

    @pl.when(is_last)
    def _():
        for m in range(2):
            end_gradient(m).start()

    barrier = pltpu.get_barrier_semaphore()
    for neighbour in (before, after):
        pl.semaphore_signal(barrier, inc=1, device_id={"section": neighbour}, device_id_type=MESH)
    pl.semaphore_wait(barrier, 2)

    for load in loads:
        load.wait()

    @pl.when(jnp.logical_not(is_first))
    def _():
        transpose_weights(r)

    @pl.loop(0, 2)
    def _(m):
        @pl.when(is_first)
        def _():
            entry(m).wait()

        @pl.when(jnp.logical_not(is_first))
        def _():
            pass_on(m).wait_recv()

        forward_step(m, r)

        @pl.when(jnp.logical_not(is_last))
        def _():
            pass_on(m).start()

        keep_output(m).start()

    @pl.when(is_first)
    def _():
        transpose_weights(r)

    for m in range(2):
        r["normed_t"][:, 128 * m : 128 * m + 128] = r["normed"][m].T
        r["mixed_t"][:, 128 * m : 128 * m + 128] = r["mixed"][m].T

    @pl.loop(0, 2)
    def _(m):
        @pl.when(is_last)
        def _():
            end_gradient(m).wait()

        @pl.when(jnp.logical_not(is_last))
        def _():
            pass_back(m).wait_recv()

        backward_step(m, r)

        @pl.when(jnp.logical_not(is_first))
        def _():
            pass_back(m).start()

        keep_gradient(m).start()

    @pl.loop(0, 12)
    def _(j):
        c = pl.ds(pl.multiple_of(256 * j, 256), 256)
        r["part_qkv"][:, c] = dg(
            r["normed_t"][...], r["gproj"][:, :, c].reshape(256, 256)
        ).astype(BF16)

    @pl.loop(0, 4)
    def _(j):
        c = pl.ds(pl.multiple_of(256 * j, 256), 256)
        r["part_out"][:, c] = dg(
            r["mixed_t"][...], r["gin"][:, :, c].reshape(256, 256)
        ).astype(BF16)

    for m in range(2):
        keep_output(m).wait()
        keep_gradient(m).wait()

        @pl.when(jnp.logical_not(is_last))
        def _():
            pass_on(m).wait_send()

        @pl.when(jnp.logical_not(is_first))
        def _():
            pass_back(m).wait_send()


def relay(patches, segments, w_qkv, w_out, cotangent):
    inputs = [
        ("patches", patches, pl.ANY),
        ("segments", segments, pltpu.VMEM),
        ("w_qkv_hbm", w_qkv, pl.ANY),
        ("w_out_hbm", w_out, pl.ANY),
        ("cotangent", cotangent, pl.ANY),
    ]
    stacked = (1,) + patches.shape
    results = [
        ("outputs", stacked, BF16, pl.ANY),
        ("input_grads", stacked, BF16, pl.ANY),
        ("part_qkv", w_qkv.shape[1:], BF16, pltpu.VMEM),
        ("part_out", w_out.shape[1:], BF16, pltpu.VMEM),
    ]
    block = (2, 128, 1024)
    scratch = [
        ("xin", pltpu.VMEM(block, BF16)),
        ("gin", pltpu.VMEM(block, BF16)),
        ("xout", pltpu.VMEM(block, BF16)),
        ("gout", pltpu.VMEM(block, BF16)),
        ("normed", pltpu.VMEM(block, BF16)),
        ("mixed", pltpu.VMEM(block, BF16)),
        ("normed_t", pltpu.VMEM((1024, 256), BF16)),
        ("mixed_t", pltpu.VMEM((1024, 256), BF16)),
        ("gproj", pltpu.VMEM((2, 128, 3072), BF16)),
        ("gn", pltpu.VMEM((128, 1024), F32)),
        ("wqkv", pltpu.VMEM((1024, 3072), BF16)),
        ("wout", pltpu.VMEM((1024, 1024), BF16)),
        ("wqkv_t", pltpu.VMEM((3072, 1024), BF16)),
        ("wout_t", pltpu.VMEM((1024, 1024), BF16)),
        ("xinv", pltpu.VMEM((2, 128, 128), F32)),
        ("qs", pltpu.VMEM((2, 8, 128, 128), BF16)),
        ("kt", pltpu.VMEM((2, 8, 128, 128), BF16)),
        ("v", pltpu.VMEM((2, 8, 128, 128), BF16)),
        ("qi", pltpu.VMEM((2, 8, 2, 128), F32)),
        ("ki", pltpu.VMEM((2, 8, 2, 128), F32)),
        ("probs", pltpu.VMEM((2, 8, 128, 256), BF16)),
        ("load", pltpu.SemaphoreType.DMA((6,))),
        ("store", pltpu.SemaphoreType.DMA((4,))),
        ("x_send", pltpu.SemaphoreType.DMA((2,))),
        ("x_recv", pltpu.SemaphoreType.DMA((2,))),
        ("g_send", pltpu.SemaphoreType.DMA((2,))),
        ("g_recv", pltpu.SemaphoreType.DMA((2,))),
    ]
    names = [i[0] for i in inputs] + [o[0] for o in results] + [s[0] for s in scratch]
    return pl.pallas_call(
        functools.partial(relay_kernel, names),
        out_shape=[jax.ShapeDtypeStruct(o[1], o[2]) for o in results],
        in_specs=[pl.BlockSpec(memory_space=i[2]) for i in inputs],
        out_specs=[pl.BlockSpec(memory_space=o[3]) for o in results],
        scratch_shapes=[s[1] for s in scratch],
        compiler_params=pltpu.CompilerParams(
            collective_id=0, has_side_effects=True, vmem_limit_bytes=58 << 20
        ),
        name="relay",
    )(*[i[1] for i in inputs])


def on_device(patches, segment_ids, weights_qkv, weights_out, cotangent):
    produced, grads, whole_qkv, whole_out = relay(
        patches, segment_ids, weights_qkv, weights_out, cotangent
    )
    total_qkv = lax.psum_scatter(whole_qkv, "dp", scatter_dimension=0, tiled=True).astype(F32)
    total_out = lax.psum_scatter(whole_out, "dp", scatter_dimension=1, tiled=True).astype(F32)
    return (produced, grads, total_qkv[None], total_out[None])


def solution(mesh):
    return jax.shard_map(
        on_device,
        mesh=mesh,
        in_specs=(
            P(None, "dp", None, None),
            P(None, "dp", None),
            P("section", None, None),
            P("section", None, None),
            P(None, "dp", None, None),
        ),
        out_specs=(
            P("section", None, "dp", None, None),
            P("section", None, "dp", None, None),
            P("section", "dp", None),
            P("section", None, "dp"),
        ),
        check_vma=False,
    )
```

```python
import functools
import types

import jax
import jax.numpy as jnp
from jax import lax
from jax.experimental import pallas as pl
from jax.experimental.pallas import tpu as pltpu
from jax.sharding import PartitionSpec as P

BF16 = jnp.bfloat16
F32 = jnp.float32
EPSILON = 1e-6
MESH = pl.DeviceIdType.MESH


def dg(a,b,ca=1,cb=0): return lax.dot_general(a,b,(((ca,),(cb,)),((),())),preferred_element_type=F32)

def block_diagonal(pair):
    blank = jnp.zeros((64, pair.shape[1]), pair.dtype)
    top = jnp.concatenate([pair[:64], blank], axis=1)
    bottom = jnp.concatenate([blank, pair[64:]], axis=1)
    return jnp.concatenate([top, bottom], axis=0)

def head_norm(rows):
    grouped = rows.reshape(2, 64, rows.shape[1])
    centred = grouped - jnp.mean(grouped, axis=1, keepdims=True)
    inverse = lax.rsqrt(jnp.mean(centred * centred, axis=1, keepdims=True) + EPSILON)
    return (centred * inverse).reshape(rows.shape), inverse[:, 0, :]

def head_norm_pull(grad, normed, inverse):
    tokens = grad.shape[1]
    g = grad.reshape(2, 64, tokens)
    n = normed.reshape(2, 64, tokens)
    first = jnp.mean(g, axis=1, keepdims=True)
    second = jnp.mean(g * n, axis=1, keepdims=True)
    return ((g - first - n * second) * inverse[:, None, :]).reshape(grad.shape)

def normalise(m, r):
    x = r.xin[m].astype(F32)
    centred = x - jnp.mean(x, axis=-1, keepdims=True)
    inverse = lax.rsqrt(jnp.mean(centred * centred, axis=-1, keepdims=True) + EPSILON)
    r.xinv[m] = jnp.broadcast_to(inverse, (128, 128))
    r.normed[m] = (centred * inverse).astype(BF16)


def attend(m, r):
    queries_in = jnp.broadcast_to(r.segments[m].astype(F32), (128, 128))
    allowed = queries_in == queries_in.T
    allowed = jnp.concatenate([allowed, allowed], axis=1)
    normed = r.normed[m]
    live = {}

    def project(quad):
        for name, start in (("q", 0), ("k", 1024), ("v", 2048)):
            column = start + 256 * quad
            live[name, quad] = dg(normed, r.wqkv[:, column : column + 256])

    def norms(quad):
        for half in range(2):
            pair = 2 * quad + half
            c = slice(128 * half, 128 * half + 128)
            q, r.qi[m, pair] = head_norm(live["q", quad][:, c].T)
            k, r.ki[m, pair] = head_norm(live["k", quad][:, c].T)
            v = live["v", quad][:, c].astype(BF16)
            qs, kt = (q * 0.125).astype(BF16), k.astype(BF16)
            r.qs[m, pair], r.kt[m, pair], r.v[m, pair] = qs, kt, v
            live["qs", pair], live["kn", pair], live["vt", pair] = qs, kt.T, v.T

    def scores(quad):
        for pair in (2 * quad, 2 * quad + 1):
            live["s", pair] = dg(live["kn", pair], block_diagonal(live["qs", pair]))

    def softmax(quad):
        for pair in (2 * quad, 2 * quad + 1):
            w = jnp.where(allowed, jnp.exp(live["s", pair]), 0.0)
            p = (w * (1.0 / jnp.sum(w, axis=0, keepdims=True))).astype(BF16)
            r.probs[m, pair] = p
            live["p", pair] = p

    def mix(quad):
        for pair in (2 * quad, 2 * quad + 1):
            vt, p = live["vt", pair], live["p", pair]
            o = [dg(vt[64 * i : 64 * i + 64], p[:, 128 * i : 128 * i + 128]) for i in range(2)]
            live["o", pair] = jnp.concatenate(o, axis=0).astype(BF16)

    def turn(quad):
        for pair in (2 * quad, 2 * quad + 1):
            r.mixed[m, :, 128 * pair : 128 * pair + 128] = live["o", pair].T

    for stage in (project, norms, scores, softmax, mix, turn):
        for quad in range(4):
            stage(quad)


def project_out(m, r):
    mixed = r.mixed[m]
    for j in range(4):
        c = slice(256*j, 256*j+256)
        branch = dg(mixed, r.wout[:, c])
        r.xout[m, :, c] = (r.xin[m, :, c].astype(F32) + branch).astype(BF16)

def attend_pull(m, r):
    g = r.gin[m]
    live = {}

    def project(quad):
        go4 = dg(g, r.wout_t[:, 256 * quad : 256 * quad + 256]).astype(BF16)
        for half in range(2):
            live["go", 2 * quad + half] = go4[:, 128 * half : 128 * half + 128].T

    def probs_pull(quad):
        for pair in (2 * quad, 2 * quad + 1):
            live["dp", pair] = dg(r.v[m, pair], block_diagonal(live["go", pair]))

    def values_pull(quad):
        for pair in (2 * quad, 2 * quad + 1):
            go, p = live["go", pair], r.probs[m, pair]
            gv = [dg(go[64 * i : 64 * i + 64], p[:, 128 * i : 128 * i + 128], 1, 1) for i in range(2)]
            live["gv", pair] = jnp.concatenate(gv, axis=0).astype(BF16)

    def scores_pull(quad):
        for pair in (2 * quad, 2 * quad + 1):
            p = r.probs[m, pair].astype(F32)
            pd = p * live["dp", pair]
            live["ds", pair] = (pd - p * jnp.sum(pd, axis=0, keepdims=True)).astype(BF16)

    def heads_pull(quad):
        for pair in (2 * quad, 2 * quad + 1):
            ds, kt, qs = live["ds", pair], r.kt[m, pair], r.qs[m, pair]
            cut = [(slice(64 * i, 64 * i + 64), slice(128 * i, 128 * i + 128)) for i in range(2)]
            live["gq", pair] = jnp.concatenate([dg(kt[i], ds[:, c]) for i, c in cut], axis=0)
            live["gk", pair] = jnp.concatenate([dg(qs[i], ds[:, c], 1, 1) for i, c in cut], axis=0)

    def norms_pull(quad):
        for pair in (2 * quad, 2 * quad + 1):
            qs, kt = r.qs[m, pair].astype(F32), r.kt[m, pair].astype(F32)
            gq = head_norm_pull(live["gq", pair] * 0.125, qs * 8.0, r.qi[m, pair])
            gk = head_norm_pull(live["gk", pair], kt, r.ki[m, pair])
            live["gq", pair], live["gk", pair] = gq.astype(BF16), gk.astype(BF16)

    def turn(quad):
        for pair in (2 * quad, 2 * quad + 1):
            for name, start in (("gq", 0), ("gk", 1024), ("gv", 2048)):
                column = start + 128 * pair
                r.gproj[m, :, column : column + 128] = live[name, pair].T

    for stage in (project, probs_pull, scores_pull, values_pull, heads_pull, norms_pull, turn):
        for quad in range(4):
            stage(quad)


def input_pull(m, r):
    gproj = r.gproj[m]
    for j in range(4):
        r.gn[:, 256*j:256*j+256] = dg(gproj, r.wqkv_t[:, 256*j:256*j+256])
    gn = r.gn[...]
    n = r.normed[m].astype(F32)
    first = jnp.mean(gn, axis=-1, keepdims=True)
    second = jnp.mean(gn * n, axis=-1, keepdims=True)
    dx = (gn - first - n * second) * r.xinv[m][:, :1]
    r.gout[m] = (r.gin[m].astype(F32) + dx).astype(BF16)

def transpose_weights(r):
    for j in range(8):
        r.wqkv_t[:, 128*j:128*j+128] = r.wqkv[128*j:128*j+128, :].T
        r.wout_t[:, 128*j:128*j+128] = r.wout[128*j:128*j+128, :].T


def spread(r, name, column, rows):
    getattr(r, name)[:, :, :, column : column + 128] = rows.T.reshape(16, 2, 32, 128)


def relay_kernel(names, *refs):
    r = types.SimpleNamespace(**dict(zip(names, refs)))
    section = lax.axis_index("section")
    last = lax.axis_size("section") - 1
    after = lax.rem(section + 1, last + 1)
    before = lax.rem(section + last, last + 1)
    is_first = section == 0
    is_last = section == last
    place = lax.axis_index("dp")
    core = lax.rem(place, 2)
    z = lax.rem(place // 2, 4)
    y = place // 8
    partner = place + 1 - 2 * core
    y_peers = [place + 8 * (lax.rem(y + k, 4) - y) for k in (1, 2, 3)]
    z_peers = [place + 2 * (lax.rem(z + k, 4) - z) for k in (1, 2, 3)]
    early = jnp.logical_or(jnp.logical_not(is_first), core == 1)

    loads = [
        pltpu.make_async_copy(r.w_qkv_hbm.at[0], r.wqkv, r.load.at[0]),
        pltpu.make_async_copy(r.w_out_hbm.at[0], r.wout, r.load.at[1]),
    ]

    def entry(m):
        return pltpu.make_async_copy(r.patches.at[m, 0], r.xin.at[m], r.load.at[2 + m])

    def end_gradient(m):
        return pltpu.make_async_copy(r.cotangent.at[m, 0], r.gin.at[m], r.load.at[4 + m])

    def pass_on(m):
        return pltpu.make_async_remote_copy(
            src_ref=r.xout.at[m], dst_ref=r.xin.at[m],
            send_sem=r.x_send.at[m], recv_sem=r.x_recv.at[m],
            device_id={"section": after}, device_id_type=MESH,
        )

    def pass_back(m):
        return pltpu.make_async_remote_copy(
            src_ref=r.gout.at[m], dst_ref=r.gin.at[m],
            send_sem=r.g_send.at[m], recv_sem=r.g_recv.at[m],
            device_id={"section": before}, device_id_type=MESH,
        )

    def keep_output(m):
        return pltpu.make_async_copy(r.xout.at[m], r.outputs.at[0, m, 0], r.store.at[m])

    def keep_gradient(m):
        return pltpu.make_async_copy(r.gout.at[m], r.input_grads.at[0, m, 0], r.store.at[2 + m])

    def share(name, m, index):
        return pltpu.make_async_remote_copy(
            src_ref=getattr(r, name).at[m], dst_ref=getattr(r, "their_" + name).at[m],
            send_sem=r.share_send.at[index, m], recv_sem=r.share_recv.at[index, m],
            device_id={"dp": partner}, device_id_type=MESH,
        )

    shared = ["normed", "mixed", "gin", "gproj"]

    def first_sum(half, j, k):
        if half == 0:
            block, peer = r.part.at[0, j, lax.rem(y + k, 4)], y_peers[k - 1]
        else:
            block, peer = r.part.at[1, j, :, lax.rem(z + k, 4)], z_peers[k - 1]
        return pltpu.make_async_remote_copy(
            src_ref=block, dst_ref=r.first.at[half, j, k - 1],
            send_sem=r.first_send.at[half, j, k - 1], recv_sem=r.first_recv.at[half, j, k - 1],
            device_id={"dp": peer}, device_id_type=MESH,
        )

    def second_sum(half, j, k):
        if half == 0:
            block, peer = r.half_sum.at[0, j, lax.rem(z + k, 4)], z_peers[k - 1]
        else:
            block, peer = r.half_sum.at[1, j, lax.rem(y + k, 4)], y_peers[k - 1]
        return pltpu.make_async_remote_copy(
            src_ref=block, dst_ref=r.second.at[half, j, k - 1],
            send_sem=r.second_send.at[half, j, k - 1], recv_sem=r.second_recv.at[half, j, k - 1],
            device_id={"dp": peer}, device_id_type=MESH,
        )

    @pl.when(is_first)
    def _():
        for m in range(2):
            entry(m).start()

    for load in loads:
        load.start()

    @pl.when(is_last)
    def _():
        for m in range(2):
            end_gradient(m).start()

    barrier = pltpu.get_barrier_semaphore()
    for neighbour in (before, after):
        pl.semaphore_signal(barrier, inc=1, device_id={"section": neighbour}, device_id_type=MESH)
    for peer in [partner] + y_peers + z_peers:
        pl.semaphore_signal(barrier, inc=1, device_id={"dp": peer}, device_id_type=MESH)

    @pl.when(early)
    def _():
        for load in loads:
            load.wait()
        transpose_weights(r)

    @pl.loop(0, 2)
    def _(m):
        @pl.when(is_first)
        def _():
            entry(m).wait()

        @pl.when(jnp.logical_not(is_first))
        def _():
            pass_on(m).wait_recv()

        normalise(m, r)

        @pl.when(jnp.logical_and(m == 0, jnp.logical_not(early)))
        def _():
            for load in loads:
                load.wait()

        attend(m, r)
        project_out(m, r)

        @pl.when(m == 0)
        def _():
            pl.semaphore_wait(barrier, 9)

        @pl.when(jnp.logical_not(is_last))
        def _():
            pass_on(m).start()

        keep_output(m).start()
        share("normed", m, 0).start()
        share("mixed", m, 1).start()

    @pl.when(jnp.logical_not(early))
    def _():
        transpose_weights(r)

    for m in range(2):
        share("normed", m, 0).wait_recv()
        share("mixed", m, 1).wait_recv()
    for m in range(2):
        spread(r, "normed_t", 128 * m, r.normed[m])
        spread(r, "normed_t", 256 + 128 * m, r.their_normed[m])

    @pl.loop(0, 2)
    def _(m):
        @pl.when(is_last)
        def _():
            end_gradient(m).wait()

        @pl.when(jnp.logical_not(is_last))
        def _():
            pass_back(m).wait_recv()

        share("gin", m, 2).start()
        attend_pull(m, r)
        share("gproj", m, 3).start()

        @pl.when(jnp.logical_not(is_first))
        def _():
            input_pull(m, r)
            pass_back(m).start()
            keep_gradient(m).start()

    for m in range(2):
        share("gproj", m, 3).wait_recv()

    def partial(half, j):
        column = 2048 * half + 512 * j
        if column < 3072:
            rows, name, c = r.normed_t, "gproj", slice(column, column + 512)
        else:
            rows, name, c = r.gin_t, "mixed", slice(column - 3072, column - 2560)
        rows = rows[:, core].reshape(512, 512)
        total = dg(rows[:, :256], getattr(r, name)[:, :, c].reshape(256, 512))
        total = total + dg(rows[:, 256:], getattr(r, "their_" + name)[:, :, c].reshape(256, 512))
        r.part[half, j] = total.astype(BF16).reshape(4, 4, 32, 512)

    pieces = [(half, j) for j in range(4) for half in range(2)]
    for half, j in pieces:
        if (half, j) == (1, 2):
            for m in range(2):
                share("gin", m, 2).wait_recv()
                spread(r, "gin_t", 128 * m, r.gin[m])
                spread(r, "gin_t", 256 + 128 * m, r.their_gin[m])
        partial(half, j)
        for k in (1, 2, 3):
            first_sum(half, j, k).start()

    @pl.when(is_first)
    def _():
        @pl.loop(0, 2)
        def _(m):
            input_pull(m, r)
            keep_gradient(m).start()

    for half, j in pieces:
        for k in (1, 2, 3):
            first_sum(half, j, k).wait_recv()
        own = r.part[half, j, y] if half == 0 else r.part[half, j, :, z]
        total = own.astype(F32)
        for k in (1, 2, 3):
            total = total + r.first[half, j, k - 1].astype(F32)
        r.half_sum[half, j] = total.astype(BF16)
        for k in (1, 2, 3):
            second_sum(half, j, k).start()

    for half, j in pieces:
        for k in (1, 2, 3):
            second_sum(half, j, k).wait_recv()
        total = r.half_sum[half, j, z if half == 0 else y].astype(F32)
        for k in (1, 2, 3):
            total = total + r.second[half, j, k - 1].astype(F32)
        column = 2048 * half + 512 * j
        if column < 3072:
            r.total_qkv[0, :, column : column + 512] = total
        else:
            r.total_out_t[:, column - 3072 : column - 2560] = total

    for half, j in pieces:
        for k in (1, 2, 3):
            first_sum(half, j, k).wait_send()
            second_sum(half, j, k).wait_send()
    for index, name in enumerate(shared):
        for m in range(2):
            share(name, m, index).wait_send()

    for m in range(2):
        keep_output(m).wait()
        keep_gradient(m).wait()

        @pl.when(jnp.logical_not(is_last))
        def _():
            pass_on(m).wait_send()

        @pl.when(jnp.logical_not(is_first))
        def _():
            pass_back(m).wait_send()


def relay(patches, segments, w_qkv, w_out, cotangent):
    inputs = [
        ("patches", patches, pl.ANY),
        ("segments", segments, pltpu.VMEM),
        ("w_qkv_hbm", w_qkv, pl.ANY),
        ("w_out_hbm", w_out, pl.ANY),
        ("cotangent", cotangent, pl.ANY),
    ]
    stacked = (1,) + patches.shape
    results = [
        ("outputs", stacked, BF16, pl.ANY),
        ("input_grads", stacked, BF16, pl.ANY),
        ("total_qkv", (1, 32, 3072), F32, pltpu.VMEM),
        ("total_out_t", (32, 1024), F32, pltpu.VMEM),
    ]
    block = (2, 128, 1024)
    scratch = [
        ("xin", pltpu.VMEM(block, BF16)),
        ("gin", pltpu.VMEM(block, BF16)),
        ("xout", pltpu.VMEM(block, BF16)),
        ("gout", pltpu.VMEM(block, BF16)),
        ("normed", pltpu.VMEM(block, BF16)),
        ("mixed", pltpu.VMEM(block, BF16)),
        ("their_normed", pltpu.VMEM(block, BF16)),
        ("their_mixed", pltpu.VMEM(block, BF16)),
        ("their_gin", pltpu.VMEM(block, BF16)),
        ("their_gproj", pltpu.VMEM((2, 128, 3072), BF16)),
        ("normed_t", pltpu.VMEM((16, 2, 32, 512), BF16)),
        ("gin_t", pltpu.VMEM((16, 2, 32, 512), BF16)),
        ("part", pltpu.VMEM((2, 4, 4, 4, 32, 512), BF16)),
        ("first", pltpu.VMEM((2, 4, 3, 4, 32, 512), BF16)),
        ("half_sum", pltpu.VMEM((2, 4, 4, 32, 512), BF16)),
        ("second", pltpu.VMEM((2, 4, 3, 32, 512), BF16)),
        ("share_send", pltpu.SemaphoreType.DMA((4, 2))),
        ("share_recv", pltpu.SemaphoreType.DMA((4, 2))),
        ("first_send", pltpu.SemaphoreType.DMA((2, 4, 3))),
        ("first_recv", pltpu.SemaphoreType.DMA((2, 4, 3))),
        ("second_send", pltpu.SemaphoreType.DMA((2, 4, 3))),
        ("second_recv", pltpu.SemaphoreType.DMA((2, 4, 3))),
        ("gproj", pltpu.VMEM((2, 128, 3072), BF16)),
        ("gn", pltpu.VMEM((128, 1024), F32)),
        ("wqkv", pltpu.VMEM((1024, 3072), BF16)),
        ("wout", pltpu.VMEM((1024, 1024), BF16)),
        ("wqkv_t", pltpu.VMEM((3072, 1024), BF16)),
        ("wout_t", pltpu.VMEM((1024, 1024), BF16)),
        ("xinv", pltpu.VMEM((2, 128, 128), F32)),
        ("qs", pltpu.VMEM((2, 8, 128, 128), BF16)),
        ("kt", pltpu.VMEM((2, 8, 128, 128), BF16)),
        ("v", pltpu.VMEM((2, 8, 128, 128), BF16)),
        ("qi", pltpu.VMEM((2, 8, 2, 128), F32)),
        ("ki", pltpu.VMEM((2, 8, 2, 128), F32)),
        ("probs", pltpu.VMEM((2, 8, 128, 256), BF16)),
        ("load", pltpu.SemaphoreType.DMA((6,))),
        ("store", pltpu.SemaphoreType.DMA((4,))),
        ("x_send", pltpu.SemaphoreType.DMA((2,))),
        ("x_recv", pltpu.SemaphoreType.DMA((2,))),
        ("g_send", pltpu.SemaphoreType.DMA((2,))),
        ("g_recv", pltpu.SemaphoreType.DMA((2,))),
    ]
    names = [i[0] for i in inputs] + [o[0] for o in results] + [s[0] for s in scratch]
    return pl.pallas_call(
        functools.partial(relay_kernel, names),
        out_shape=[jax.ShapeDtypeStruct(o[1], o[2]) for o in results],
        in_specs=[pl.BlockSpec(memory_space=i[2]) for i in inputs],
        out_specs=[pl.BlockSpec(memory_space=o[3]) for o in results],
        scratch_shapes=[s[1] for s in scratch],
        compiler_params=pltpu.CompilerParams(
            collective_id=0, has_side_effects=True, vmem_limit_bytes=58 << 20
        ),
        name="relay",
    )(*[i[1] for i in inputs])


def settle_kernel(count, *refs):
    sources, targets, held = refs[:count], refs[count : 2 * count], refs[2 * count : 3 * count]
    read, written = refs[-2:]
    into = [pltpu.make_async_copy(a, b, read.at[i]) for i, (a, b) in enumerate(zip(sources, held))]
    out = [pltpu.make_async_copy(a, b, written.at[i]) for i, (a, b) in enumerate(zip(held, targets))]
    for copy in into:
        copy.start()
    for first, second in zip(into, out):
        first.wait()
        second.start()
    for copy in out:
        copy.wait()


def settle(arrays):
    return pl.pallas_call(
        functools.partial(settle_kernel, len(arrays)),
        out_shape=[jax.ShapeDtypeStruct(a.shape, a.dtype) for a in arrays],
        in_specs=[pl.BlockSpec(memory_space=pl.ANY)] * len(arrays),
        out_specs=[pl.BlockSpec(memory_space=pl.ANY)] * len(arrays),
        scratch_shapes=[pltpu.VMEM(a.shape, a.dtype) for a in arrays]
        + [pltpu.SemaphoreType.DMA((len(arrays),))] * 2,
        name="settle",
    )(*arrays)


def on_device(patches, segment_ids, weights_qkv, weights_out, cotangent):
    produced, grads, total_qkv, total_out_t = settle(
        relay(patches, segment_ids, weights_qkv, weights_out, cotangent)
    )
    return (produced, grads, total_qkv, total_out_t.T[None])


def solution(mesh):
    return jax.shard_map(
        on_device,
        mesh=mesh,
        in_specs=(
            P(None, "dp", None, None),
            P(None, "dp", None),
            P("section", None, None),
            P("section", None, None),
            P(None, "dp", None, None),
        ),
        out_specs=(
            P("section", None, "dp", None, None),
            P("section", None, "dp", None, None),
            P("section", "dp", None),
            P("section", None, "dp"),
        ),
        check_vma=False,
    )
```

```python
import functools
import types

import jax
import jax.numpy as jnp
from jax import lax
from jax.experimental import pallas as pl
from jax.experimental.pallas import tpu as pltpu
from jax.sharding import PartitionSpec as P

BF16 = jnp.bfloat16
F32 = jnp.float32
EPSILON = 1e-6
MESH = pl.DeviceIdType.MESH


def dg(a,b,ca=1,cb=0): return lax.dot_general(a,b,(((ca,),(cb,)),((),())),preferred_element_type=F32)

def block_diagonal(pair):
    blank = jnp.zeros((64, pair.shape[1]), pair.dtype)
    top = jnp.concatenate([pair[:64], blank], axis=1)
    bottom = jnp.concatenate([blank, pair[64:]], axis=1)
    return jnp.concatenate([top, bottom], axis=0)

def head_norm(rows):
    grouped = rows.reshape(2, 64, rows.shape[1])
    centred = grouped - jnp.mean(grouped, axis=1, keepdims=True)
    inverse = lax.rsqrt(jnp.mean(centred * centred, axis=1, keepdims=True) + EPSILON)
    return (centred * inverse).reshape(rows.shape), inverse[:, 0, :]

def head_norm_pull(grad, normed, inverse):
    tokens = grad.shape[1]
    g = grad.reshape(2, 64, tokens)
    n = normed.reshape(2, 64, tokens)
    first = jnp.mean(g, axis=1, keepdims=True)
    second = jnp.mean(g * n, axis=1, keepdims=True)
    return ((g - first - n * second) * inverse[:, None, :]).reshape(grad.shape)

def normalise(m, r):
    x = r.xin[m].astype(F32)
    centred = x - jnp.mean(x, axis=-1, keepdims=True)
    inverse = lax.rsqrt(jnp.mean(centred * centred, axis=-1, keepdims=True) + EPSILON)
    r.xinv[m] = jnp.broadcast_to(inverse, (128, 128))
    r.normed[m] = (centred * inverse).astype(BF16)


def attend(m, r):
    queries_in = jnp.broadcast_to(r.segments[m].astype(F32), (128, 128))
    allowed = queries_in == queries_in.T
    allowed = jnp.concatenate([allowed, allowed], axis=1)
    normed = r.normed[m]
    live = {}

    def project(quad):
        for name, start in (("q", 0), ("k", 1024), ("v", 2048)):
            column = start + 256 * quad
            live[name, quad] = dg(normed, r.wqkv[:, column : column + 256])

    def norms(quad):
        for half in range(2):
            pair = 2 * quad + half
            c = slice(128 * half, 128 * half + 128)
            q, r.qi[m, pair] = head_norm(live["q", quad][:, c].T)
            k, r.ki[m, pair] = head_norm(live["k", quad][:, c].T)
            v = live["v", quad][:, c].astype(BF16)
            qs, kt = (q * 0.125).astype(BF16), k.astype(BF16)
            r.qs[m, pair], r.kt[m, pair], r.v[m, pair] = qs, kt, v
            live["qs", pair], live["kn", pair], live["vt", pair] = qs, kt.T, v.T

    def scores(quad):
        for pair in (2 * quad, 2 * quad + 1):
            live["s", pair] = dg(live["kn", pair], block_diagonal(live["qs", pair]))

    def softmax(quad):
        for pair in (2 * quad, 2 * quad + 1):
            w = jnp.where(allowed, jnp.exp(live["s", pair]), 0.0)
            p = (w * (1.0 / jnp.sum(w, axis=0, keepdims=True))).astype(BF16)
            r.probs[m, pair] = p
            live["p", pair] = p

    def mix(quad):
        for pair in (2 * quad, 2 * quad + 1):
            vt, p = live["vt", pair], live["p", pair]
            o = [dg(vt[64 * i : 64 * i + 64], p[:, 128 * i : 128 * i + 128]) for i in range(2)]
            live["o", pair] = jnp.concatenate(o, axis=0).astype(BF16)

    def turn(quad):
        for pair in (2 * quad, 2 * quad + 1):
            r.mixed[m, :, 128 * pair : 128 * pair + 128] = live["o", pair].T

    for stage in (project, norms, scores, softmax, mix, turn):
        for quad in range(4):
            stage(quad)


def project_out(m, r):
    mixed = r.mixed[m]
    for j in range(4):
        c = slice(256*j, 256*j+256)
        branch = dg(mixed, r.wout[:, c])
        r.xout[m, :, c] = (r.xin[m, :, c].astype(F32) + branch).astype(BF16)

def attend_pull(m, r):
    g = r.gin[m]
    live = {}

    def project(quad):
        go4 = dg(g, r.wout_t[:, 256 * quad : 256 * quad + 256]).astype(BF16)
        for half in range(2):
            live["go", 2 * quad + half] = go4[:, 128 * half : 128 * half + 128].T

    def probs_pull(quad):
        for pair in (2 * quad, 2 * quad + 1):
            live["dp", pair] = dg(r.v[m, pair], block_diagonal(live["go", pair]))

    def values_pull(quad):
        for pair in (2 * quad, 2 * quad + 1):
            go, p = live["go", pair], r.probs[m, pair]
            gv = [dg(go[64 * i : 64 * i + 64], p[:, 128 * i : 128 * i + 128], 1, 1) for i in range(2)]
            live["gv", pair] = jnp.concatenate(gv, axis=0).astype(BF16)

    def scores_pull(quad):
        for pair in (2 * quad, 2 * quad + 1):
            p = r.probs[m, pair].astype(F32)
            pd = p * live["dp", pair]
            live["ds", pair] = (pd - p * jnp.sum(pd, axis=0, keepdims=True)).astype(BF16)

    def heads_pull(quad):
        for pair in (2 * quad, 2 * quad + 1):
            ds, kt, qs = live["ds", pair], r.kt[m, pair], r.qs[m, pair]
            cut = [(slice(64 * i, 64 * i + 64), slice(128 * i, 128 * i + 128)) for i in range(2)]
            live["gq", pair] = jnp.concatenate([dg(kt[i], ds[:, c]) for i, c in cut], axis=0)
            live["gk", pair] = jnp.concatenate([dg(qs[i], ds[:, c], 1, 1) for i, c in cut], axis=0)

    def norms_pull(quad):
        for pair in (2 * quad, 2 * quad + 1):
            qs, kt = r.qs[m, pair].astype(F32), r.kt[m, pair].astype(F32)
            gq = head_norm_pull(live["gq", pair] * 0.125, qs * 8.0, r.qi[m, pair])
            gk = head_norm_pull(live["gk", pair], kt, r.ki[m, pair])
            live["gq", pair], live["gk", pair] = gq.astype(BF16), gk.astype(BF16)

    def turn(quad):
        for pair in (2 * quad, 2 * quad + 1):
            for name, start in (("gq", 0), ("gk", 1024), ("gv", 2048)):
                column = start + 128 * pair
                r.gproj[m, :, column : column + 128] = live[name, pair].T

    for stage in (project, probs_pull, scores_pull, values_pull, heads_pull, norms_pull, turn):
        for quad in range(4):
            stage(quad)


def input_pull(m, r):
    gproj = r.gproj[m]
    for j in range(4):
        r.gn[:, 256*j:256*j+256] = dg(gproj, r.wqkv_t[:, 256*j:256*j+256])
    gn = r.gn[...]
    n = r.normed[m].astype(F32)
    first = jnp.mean(gn, axis=-1, keepdims=True)
    second = jnp.mean(gn * n, axis=-1, keepdims=True)
    dx = (gn - first - n * second) * r.xinv[m][:, :1]
    r.gout[m] = (r.gin[m].astype(F32) + dx).astype(BF16)

def transpose_weights(r):
    for j in range(8):
        r.wqkv_t[:, 128*j:128*j+128] = r.wqkv[128*j:128*j+128, :].T
        r.wout_t[:, 128*j:128*j+128] = r.wout[128*j:128*j+128, :].T


def spread(r, name, column, rows):
    getattr(r, name)[:, :, :, column : column + 128] = rows.T.reshape(16, 2, 32, 128)


def swap(p, mask):
    if mask == 1:
        return p + 1 - 2 * lax.rem(p, 2)
    if mask == 2:
        return lax.rem(p + 2, 4)
    return 3 - p


def relay_kernel(names, *refs):
    r = types.SimpleNamespace(**dict(zip(names, refs)))
    section = lax.axis_index("section")
    last = lax.axis_size("section") - 1
    after = lax.rem(section + 1, last + 1)
    before = lax.rem(section + last, last + 1)
    is_first = section == 0
    is_last = section == last
    place = lax.axis_index("dp")
    core = lax.rem(place, 2)
    z = lax.rem(place // 2, 4)
    y = place // 8
    partner = place + 1 - 2 * core
    y_peers = {a: place + 8 * (swap(y, a) - y) for a in (1, 3)}
    z_peers = {a: place + 2 * (swap(z, a) - z) for a in (1, 3)}
    early = jnp.logical_or(jnp.logical_not(is_first), core == 1)

    loads = [
        pltpu.make_async_copy(r.w_qkv_hbm.at[0], r.wqkv, r.load.at[0]),
        pltpu.make_async_copy(r.w_out_hbm.at[0], r.wout, r.load.at[1]),
    ]

    def entry(m):
        return pltpu.make_async_copy(r.patches.at[m, 0], r.xin.at[m], r.load.at[2 + m])

    def end_gradient(m):
        return pltpu.make_async_copy(r.cotangent.at[m, 0], r.gin.at[m], r.load.at[4 + m])

    def pass_on(m):
        return pltpu.make_async_remote_copy(
            src_ref=r.xout.at[m], dst_ref=r.xin.at[m],
            send_sem=r.x_send.at[m], recv_sem=r.x_recv.at[m],
            device_id={"section": after}, device_id_type=MESH,
        )

    def pass_back(m):
        return pltpu.make_async_remote_copy(
            src_ref=r.gout.at[m], dst_ref=r.gin.at[m],
            send_sem=r.g_send.at[m], recv_sem=r.g_recv.at[m],
            device_id={"section": before}, device_id_type=MESH,
        )

    def keep_output(m):
        return pltpu.make_async_copy(r.xout.at[m], r.outputs.at[0, m, 0], r.store.at[m])

    def keep_gradient(m):
        return pltpu.make_async_copy(r.gout.at[m], r.input_grads.at[0, m, 0], r.store.at[2 + m])

    def share(name, m, index):
        return pltpu.make_async_remote_copy(
            src_ref=getattr(r, name).at[m], dst_ref=getattr(r, "their_" + name).at[m],
            send_sem=r.share_send.at[index, m], recv_sem=r.share_recv.at[index, m],
            device_id={"dp": partner}, device_id_type=MESH,
        )

    shared = ["normed", "mixed", "gin", "gproj"]

    def axes(half):
        return ((y, y_peers), (z, z_peers)) if half == 0 else ((z, z_peers), (y, y_peers))

    def masks(j):
        return (1, 3) if j % 2 == 0 else (3, 1)

    def block(half, j, position):
        return r.part.at[0, j, position] if half == 0 else r.part.at[1, j, :, position]

    def send(half, j, step):
        (p, p_peers), (q, q_peers) = axes(half)
        a, b = masks(j)
        if step == 0:
            source, target, peer = block(half, j, swap(p, 2)), r.far_in, p_peers[a]
        elif step == 1:
            source, target, peer = block(half, j, swap(p, a)), r.near_in, p_peers[a]
        elif step == 2:
            source, target, peer = r.far_sum.at[half, j], r.last_in, p_peers[b]
        elif step == 3:
            source, target, peer = r.row.at[half, j, swap(q, 2)], r.row_far_in, q_peers[a]
        elif step == 4:
            source, target, peer = r.row.at[half, j, swap(q, a)], r.row_near_in, q_peers[a]
        else:
            source, target, peer = r.row_far_sum.at[half, j], r.row_last_in, q_peers[b]
        return pltpu.make_async_remote_copy(
            src_ref=source, dst_ref=target.at[half, j],
            send_sem=r.sum_send.at[half, j, step], recv_sem=r.sum_recv.at[half, j, step],
            device_id={"dp": peer}, device_id_type=MESH,
        )

    def sum_one(half, j):
        (p, _), _ = axes(half)
        send(half, j, 0).wait_recv()
        held = block(half, j, swap(p, masks(j)[1]))[...].astype(F32)
        r.far_sum[half, j] = (held + r.far_in[half, j].astype(F32)).astype(BF16)
        send(half, j, 2).start()

    def sum_two(half, j):
        (p, _), _ = axes(half)
        send(half, j, 1).wait_recv()
        send(half, j, 2).wait_recv()
        total = block(half, j, p)[...].astype(F32) + r.near_in[half, j].astype(F32)
        r.row[half, j] = (total + r.last_in[half, j].astype(F32)).astype(BF16)
        send(half, j, 3).start()
        send(half, j, 4).start()

    def sum_three(half, j):
        _, (q, _) = axes(half)
        send(half, j, 3).wait_recv()
        held = r.row[half, j, swap(q, masks(j)[1])].astype(F32)
        r.row_far_sum[half, j] = (held + r.row_far_in[half, j].astype(F32)).astype(BF16)
        send(half, j, 5).start()

    def sum_four(half, j):
        _, (q, _) = axes(half)
        send(half, j, 4).wait_recv()
        send(half, j, 5).wait_recv()
        total = r.row[half, j, q].astype(F32) + r.row_near_in[half, j].astype(F32)
        total = total + r.row_last_in[half, j].astype(F32)
        column = 2048 * half + 512 * j
        if column < 3072:
            r.total_qkv[0, :, column : column + 512] = total
        else:
            r.total_out_t[:, column - 3072 : column - 2560] = total

    @pl.when(is_first)
    def _():
        for m in range(2):
            entry(m).start()

    for load in loads:
        load.start()

    @pl.when(is_last)
    def _():
        for m in range(2):
            end_gradient(m).start()

    barrier = pltpu.get_barrier_semaphore()
    for neighbour in (before, after):
        pl.semaphore_signal(barrier, inc=1, device_id={"section": neighbour}, device_id_type=MESH)
    for peer in [partner, *y_peers.values(), *z_peers.values()]:
        pl.semaphore_signal(barrier, inc=1, device_id={"dp": peer}, device_id_type=MESH)

    @pl.when(early)
    def _():
        for load in loads:
            load.wait()
        transpose_weights(r)

    def forward(m):
        @pl.when(is_first)
        def _():
            entry(m).wait()

        @pl.when(jnp.logical_not(is_first))
        def _():
            pass_on(m).wait_recv()

        normalise(m, r)

        @pl.when(jnp.logical_and(m == 0, jnp.logical_not(early)))
        def _():
            for load in loads:
                load.wait()

        attend(m, r)
        project_out(m, r)

        @pl.when(m == 0)
        def _():
            pl.semaphore_wait(barrier, 7)

        @pl.when(jnp.logical_not(is_last))
        def _():
            pass_on(m).start()

        keep_output(m).start()
        share("normed", m, 0).start()
        share("mixed", m, 1).start()

    def spread_normed():
        for m in range(2):
            share("normed", m, 0).wait_recv()
            share("mixed", m, 1).wait_recv()
        for m in range(2):
            spread(r, "normed_t", 128 * m, r.normed[m])
            spread(r, "normed_t", 256 + 128 * m, r.their_normed[m])

    def backward(m):
        @pl.when(jnp.logical_and(m == 0, jnp.logical_not(early)))
        def _():
            transpose_weights(r)

        @pl.when(jnp.logical_and(m == 0, is_first))
        def _():
            spread_normed()

        @pl.when(is_last)
        def _():
            end_gradient(m).wait()

        @pl.when(jnp.logical_not(is_last))
        def _():
            pass_back(m).wait_recv()

        share("gin", m, 2).start()
        attend_pull(m, r)
        share("gproj", m, 3).start()

        @pl.when(jnp.logical_not(is_first))
        def _():
            input_pull(m, r)
            pass_back(m).start()
            keep_gradient(m).start()

    turns = section // last

    @pl.loop(0, 4)
    def _(t):
        back = turns * lax.rem(t, 2) + (1 - turns) * (t // 2)
        m = turns * (t // 2) + (1 - turns) * lax.rem(t, 2)

        @pl.when(back == 0)
        def _():
            forward(m)

        @pl.when(back == 1)
        def _():
            backward(m)

    @pl.when(jnp.logical_not(is_first))
    def _():
        spread_normed()

    for m in range(2):
        share("gproj", m, 3).wait_recv()

    def partial(half, j):
        column = 2048 * half + 512 * j
        if column < 3072:
            rows, name, c = r.normed_t, "gproj", slice(column, column + 512)
        else:
            rows, name, c = r.gin_t, "mixed", slice(column - 3072, column - 2560)
        rows = rows[:, core].reshape(512, 512)
        total = dg(rows[:, :256], getattr(r, name)[:, :, c].reshape(256, 512))
        total = total + dg(rows[:, 256:], getattr(r, "their_" + name)[:, :, c].reshape(256, 512))
        r.part[half, j] = total.astype(BF16).reshape(4, 4, 32, 512)

    pieces = [(half, j) for j in range(4) for half in range(2)]
    for half, j in pieces:
        if (half, j) == (1, 2):
            for m in range(2):
                share("gin", m, 2).wait_recv()
                spread(r, "gin_t", 128 * m, r.gin[m])
                spread(r, "gin_t", 256 + 128 * m, r.their_gin[m])
        partial(half, j)
        send(half, j, 0).start()
        send(half, j, 1).start()

    @pl.when(is_first)
    def _():
        @pl.loop(0, 2)
        def _(m):
            input_pull(m, r)
            keep_gradient(m).start()

    stages = (sum_one, sum_two, sum_three, sum_four)
    lags = (0, 3, 6, 9)
    for step in range(len(pieces) + lags[-1]):
        for lag, stage in zip(lags, stages):
            if 0 <= step - lag < len(pieces):
                stage(*pieces[step - lag])

    for half, j in pieces:
        for step in range(6):
            send(half, j, step).wait_send()
    for index, name in enumerate(shared):
        for m in range(2):
            share(name, m, index).wait_send()

    for m in range(2):
        keep_output(m).wait()
        keep_gradient(m).wait()

        @pl.when(jnp.logical_not(is_last))
        def _():
            pass_on(m).wait_send()

        @pl.when(jnp.logical_not(is_first))
        def _():
            pass_back(m).wait_send()


def relay(patches, segments, w_qkv, w_out, cotangent):
    inputs = [
        ("patches", patches, pl.ANY),
        ("segments", segments, pltpu.VMEM),
        ("w_qkv_hbm", w_qkv, pl.ANY),
        ("w_out_hbm", w_out, pl.ANY),
        ("cotangent", cotangent, pl.ANY),
    ]
    stacked = (1,) + patches.shape
    results = [
        ("outputs", stacked, BF16, pl.ANY),
        ("input_grads", stacked, BF16, pl.ANY),
        ("total_qkv", (1, 32, 3072), F32, pltpu.VMEM),
        ("total_out_t", (32, 1024), F32, pltpu.VMEM),
    ]
    block = (2, 128, 1024)
    scratch = [
        ("xin", pltpu.VMEM(block, BF16)),
        ("gin", pltpu.VMEM(block, BF16)),
        ("xout", pltpu.VMEM(block, BF16)),
        ("gout", pltpu.VMEM(block, BF16)),
        ("normed", pltpu.VMEM(block, BF16)),
        ("mixed", pltpu.VMEM(block, BF16)),
        ("their_normed", pltpu.VMEM(block, BF16)),
        ("their_mixed", pltpu.VMEM(block, BF16)),
        ("their_gin", pltpu.VMEM(block, BF16)),
        ("their_gproj", pltpu.VMEM((2, 128, 3072), BF16)),
        ("normed_t", pltpu.VMEM((16, 2, 32, 512), BF16)),
        ("gin_t", pltpu.VMEM((16, 2, 32, 512), BF16)),
        ("part", pltpu.VMEM((2, 4, 4, 4, 32, 512), BF16)),
        *((name, pltpu.VMEM((2, 4, 4, 32, 512), BF16)) for name in ("far_in", "near_in", "far_sum", "last_in", "row")),
        *((name, pltpu.VMEM((2, 4, 32, 512), BF16)) for name in ("row_far_in", "row_near_in", "row_far_sum", "row_last_in")),
        ("sum_send", pltpu.SemaphoreType.DMA((2, 4, 6))),
        ("sum_recv", pltpu.SemaphoreType.DMA((2, 4, 6))),
        ("share_send", pltpu.SemaphoreType.DMA((4, 2))),
        ("share_recv", pltpu.SemaphoreType.DMA((4, 2))),
        ("gproj", pltpu.VMEM((2, 128, 3072), BF16)),
        ("gn", pltpu.VMEM((128, 1024), F32)),
        ("wqkv", pltpu.VMEM((1024, 3072), BF16)),
        ("wout", pltpu.VMEM((1024, 1024), BF16)),
        ("wqkv_t", pltpu.VMEM((3072, 1024), BF16)),
        ("wout_t", pltpu.VMEM((1024, 1024), BF16)),
        ("xinv", pltpu.VMEM((2, 128, 128), F32)),
        ("qs", pltpu.VMEM((2, 8, 128, 128), BF16)),
        ("kt", pltpu.VMEM((2, 8, 128, 128), BF16)),
        ("v", pltpu.VMEM((2, 8, 128, 128), BF16)),
        ("qi", pltpu.VMEM((2, 8, 2, 128), F32)),
        ("ki", pltpu.VMEM((2, 8, 2, 128), F32)),
        ("probs", pltpu.VMEM((2, 8, 128, 256), BF16)),
        ("load", pltpu.SemaphoreType.DMA((6,))),
        ("store", pltpu.SemaphoreType.DMA((4,))),
        ("x_send", pltpu.SemaphoreType.DMA((2,))),
        ("x_recv", pltpu.SemaphoreType.DMA((2,))),
        ("g_send", pltpu.SemaphoreType.DMA((2,))),
        ("g_recv", pltpu.SemaphoreType.DMA((2,))),
    ]
    names = [i[0] for i in inputs] + [o[0] for o in results] + [s[0] for s in scratch]
    return pl.pallas_call(
        functools.partial(relay_kernel, names),
        out_shape=[jax.ShapeDtypeStruct(o[1], o[2]) for o in results],
        in_specs=[pl.BlockSpec(memory_space=i[2]) for i in inputs],
        out_specs=[pl.BlockSpec(memory_space=o[3]) for o in results],
        scratch_shapes=[s[1] for s in scratch],
        compiler_params=pltpu.CompilerParams(
            collective_id=0, has_side_effects=True, vmem_limit_bytes=58 << 20
        ),
        name="relay",
    )(*[i[1] for i in inputs])


def settle_kernel(count, *refs):
    sources, targets, held = refs[:count], refs[count : 2 * count], refs[2 * count : 3 * count]
    read, written = refs[-2:]
    into = [pltpu.make_async_copy(a, b, read.at[i]) for i, (a, b) in enumerate(zip(sources, held))]
    out = [pltpu.make_async_copy(a, b, written.at[i]) for i, (a, b) in enumerate(zip(held, targets))]
    for copy in into:
        copy.start()
    for first, second in zip(into, out):
        first.wait()
        second.start()
    for copy in out:
        copy.wait()


def settle(arrays):
    return pl.pallas_call(
        functools.partial(settle_kernel, len(arrays)),
        out_shape=[jax.ShapeDtypeStruct(a.shape, a.dtype) for a in arrays],
        in_specs=[pl.BlockSpec(memory_space=pl.ANY)] * len(arrays),
        out_specs=[pl.BlockSpec(memory_space=pl.ANY)] * len(arrays),
        scratch_shapes=[pltpu.VMEM(a.shape, a.dtype) for a in arrays]
        + [pltpu.SemaphoreType.DMA((len(arrays),))] * 2,
        name="settle",
    )(*arrays)


def on_device(patches, segment_ids, weights_qkv, weights_out, cotangent):
    produced, grads, total_qkv, total_out_t = settle(
        relay(patches, segment_ids, weights_qkv, weights_out, cotangent)
    )
    return (produced, grads, total_qkv, total_out_t.T[None])


def solution(mesh):
    return jax.shard_map(
        on_device,
        mesh=mesh,
        in_specs=(
            P(None, "dp", None, None),
            P(None, "dp", None),
            P("section", None, None),
            P("section", None, None),
            P(None, "dp", None, None),
        ),
        out_specs=(
            P("section", None, "dp", None, None),
            P("section", None, "dp", None, None),
            P("section", "dp", None),
            P("section", None, "dp"),
        ),
        check_vma=False,
    )
```

```python
import functools
import types

import jax
import jax.numpy as jnp
from jax import lax
from jax.experimental import pallas as pl
from jax.experimental.pallas import tpu as pltpu
from jax.sharding import PartitionSpec as P

BF16 = jnp.bfloat16
F32 = jnp.float32
EPSILON = 1e-6
MESH = pl.DeviceIdType.MESH
CHUNKS = (slice(0, 768), slice(768, 1024))
HEAD, TAIL = CHUNKS


def dg(a,b,ca=1,cb=0): return lax.dot_general(a,b,(((ca,),(cb,)),((),())),preferred_element_type=F32)

def block_diagonal(pair):
    blank = jnp.zeros((64, pair.shape[1]), pair.dtype)
    top = jnp.concatenate([pair[:64], blank], axis=1)
    bottom = jnp.concatenate([blank, pair[64:]], axis=1)
    return jnp.concatenate([top, bottom], axis=0)

def head_norm(rows):
    grouped = rows.reshape(2, 64, rows.shape[1])
    centred = grouped - jnp.mean(grouped, axis=1, keepdims=True)
    inverse = lax.rsqrt(jnp.mean(centred * centred, axis=1, keepdims=True) + EPSILON)
    return (centred * inverse).reshape(rows.shape), inverse[:, 0, :]

def head_norm_pull(grad, normed, inverse):
    tokens = grad.shape[1]
    g = grad.reshape(2, 64, tokens)
    n = normed.reshape(2, 64, tokens)
    first = jnp.mean(g, axis=1, keepdims=True)
    second = jnp.mean(g * n, axis=1, keepdims=True)
    return ((g - first - n * second) * inverse[:, None, :]).reshape(grad.shape)

def normalise(m, r):
    x = r.xin[m].astype(F32)
    average = jnp.mean(x, axis=-1, keepdims=True)
    centred = x - average
    inverse = lax.rsqrt(jnp.mean(centred * centred, axis=-1, keepdims=True) + EPSILON)
    r.xinv[m] = jnp.broadcast_to(inverse, (128, 128))
    r.normed[m] = (centred * inverse).astype(BF16)
    return average, inverse


def project_head(m, kind, r):
    for j in range(6):
        c = slice(512 * j, 512 * j + 512)
        r.begun[:, c] = dg(r.acts[kind, m, :, HEAD], r.wqkv[HEAD, c])


def attend(m, kind, r):
    queries_in = jnp.broadcast_to(r.segments[m].astype(F32), (128, 128))
    allowed = queries_in == queries_in.T
    allowed = jnp.concatenate([allowed, allowed], axis=1)
    rest = r.acts[kind, m, :, TAIL]
    raw = 1.0 - kind.astype(F32)
    average, inverse = normalise(m, r)
    average = average * raw
    inverse = inverse * raw + (1.0 - raw)
    live = {}

    def project(quad):
        for name, start in (("q", 0), ("k", 1024), ("v", 2048)):
            column = start + 256 * quad
            c = slice(column, column + 256)
            product = r.begun[:, c] + dg(rest, r.wqkv[TAIL, c])
            live[name, quad] = (product - average * r.columns[:1, c]) * inverse

    def norms(quad):
        for half in range(2):
            pair = 2 * quad + half
            c = slice(128 * half, 128 * half + 128)
            q, r.qi[m, pair] = head_norm(live["q", quad][:, c].T)
            k, r.ki[m, pair] = head_norm(live["k", quad][:, c].T)
            v = live["v", quad][:, c].astype(BF16)
            qs, kt = (q * 0.125).astype(BF16), k.astype(BF16)
            r.qs[m, pair], r.kt[m, pair], r.v[m, pair] = qs, kt, v
            live["qs", pair], live["kn", pair], live["vt", pair] = qs, kt.T, v.T

    def scores(quad):
        for pair in (2 * quad, 2 * quad + 1):
            live["s", pair] = dg(live["kn", pair], block_diagonal(live["qs", pair]))

    def softmax(quad):
        for pair in (2 * quad, 2 * quad + 1):
            w = jnp.where(allowed, jnp.exp(live["s", pair]), 0.0)
            p = (w * (1.0 / jnp.sum(w, axis=0, keepdims=True))).astype(BF16)
            r.probs[m, pair] = p
            live["p", pair] = p

    def mix(quad):
        for pair in (2 * quad, 2 * quad + 1):
            vt, p = live["vt", pair], live["p", pair]
            o = [dg(vt[64 * i : 64 * i + 64], p[:, 128 * i : 128 * i + 128]) for i in range(2)]
            live["o", pair] = jnp.concatenate(o, axis=0).astype(BF16)

    def turn(quad):
        for pair in (2 * quad, 2 * quad + 1):
            r.mixed[m, :, 128 * pair : 128 * pair + 128] = live["o", pair].T

    for stage in (project, norms, scores, softmax, mix, turn):
        for quad in range(4):
            stage(quad)


def project_out(m, r, chunk):
    mixed = r.mixed[m]
    for start in range(chunk.start, chunk.stop, 256):
        c = slice(start, start + 256)
        branch = dg(mixed, r.wout[:, c])
        r.xout[m, :, c] = (r.xin[m, :, c].astype(F32) + branch).astype(BF16)


def mixed_pull_head(m, r):
    for j in range(4):
        c = slice(256 * j, 256 * j + 256)
        r.gn[:, c] = dg(r.gin[m, :, HEAD], r.wout_t[HEAD, c])


def attend_pull(m, r):
    rest = r.gin[m, :, TAIL]
    live = {}

    def project(quad):
        c = slice(256 * quad, 256 * quad + 256)
        go4 = (r.gn[:, c] + dg(rest, r.wout_t[TAIL, c])).astype(BF16)
        for half in range(2):
            live["go", 2 * quad + half] = go4[:, 128 * half : 128 * half + 128].T

    def probs_pull(quad):
        for pair in (2 * quad, 2 * quad + 1):
            live["dp", pair] = dg(r.v[m, pair], block_diagonal(live["go", pair]))

    def values_pull(quad):
        for pair in (2 * quad, 2 * quad + 1):
            go, p = live["go", pair], r.probs[m, pair]
            gv = [dg(go[64 * i : 64 * i + 64], p[:, 128 * i : 128 * i + 128], 1, 1) for i in range(2)]
            live["gv", pair] = jnp.concatenate(gv, axis=0).astype(BF16)

    def scores_pull(quad):
        for pair in (2 * quad, 2 * quad + 1):
            p = r.probs[m, pair].astype(F32)
            pd = p * live["dp", pair]
            live["ds", pair] = (pd - p * jnp.sum(pd, axis=0, keepdims=True)).astype(BF16)

    def heads_pull(quad):
        for pair in (2 * quad, 2 * quad + 1):
            ds, kt, qs = live["ds", pair], r.kt[m, pair], r.qs[m, pair]
            cut = [(slice(64 * i, 64 * i + 64), slice(128 * i, 128 * i + 128)) for i in range(2)]
            live["gq", pair] = jnp.concatenate([dg(kt[i], ds[:, c]) for i, c in cut], axis=0)
            live["gk", pair] = jnp.concatenate([dg(qs[i], ds[:, c], 1, 1) for i, c in cut], axis=0)

    def norms_pull(quad):
        for pair in (2 * quad, 2 * quad + 1):
            qs, kt = r.qs[m, pair].astype(F32), r.kt[m, pair].astype(F32)
            gq = head_norm_pull(live["gq", pair] * 0.125, qs * 8.0, r.qi[m, pair])
            gk = head_norm_pull(live["gk", pair], kt, r.ki[m, pair])
            live["gq", pair], live["gk", pair] = gq.astype(BF16), gk.astype(BF16)

    def turn(quad):
        for pair in (2 * quad, 2 * quad + 1):
            for name, start in (("gq", 0), ("gk", 1024), ("gv", 2048)):
                column = start + 128 * pair
                r.gproj[m, :, column : column + 128] = live[name, pair].T

    for stage in (project, probs_pull, scores_pull, values_pull, heads_pull, norms_pull, turn):
        for quad in range(4):
            stage(quad)


def input_pull(m, r):
    gproj = r.gproj[m]
    for j in range(4):
        r.gn[:, 256*j:256*j+256] = dg(gproj, r.wqkv_t[:, 256*j:256*j+256])
    gn = r.gn[...]
    n = r.normed[m].astype(F32)
    first = jnp.mean(gn, axis=-1, keepdims=True)
    second = jnp.mean(gn * n, axis=-1, keepdims=True)
    dx = (gn - first - n * second) * r.xinv[m][:, :1]
    r.gout[m] = (r.gin[m].astype(F32) + dx).astype(BF16)

def transpose_weights(r):
    for j in range(8):
        r.wqkv_t[:, 128*j:128*j+128] = r.wqkv[128*j:128*j+128, :].T
        r.wout_t[:, 128*j:128*j+128] = r.wout[128*j:128*j+128, :].T
    for j in range(6):
        c = slice(512 * j, 512 * j + 512)
        r.columns[:, c] = dg(jnp.ones((16, 1024), BF16), r.wqkv[:, c])


def spread(r, name, column, rows):
    getattr(r, name)[:, :, :, column : column + 128] = rows.T.reshape(16, 2, 32, 128)


def swap(p, mask):
    if mask == 1:
        return p + 1 - 2 * lax.rem(p, 2)
    if mask == 2:
        return lax.rem(p + 2, 4)
    return 3 - p


def relay_kernel(names, *refs):
    r = types.SimpleNamespace(**dict(zip(names, refs)))
    r.xin, r.normed = r.acts.at[0], r.acts.at[1]
    section = lax.axis_index("section")
    last = lax.axis_size("section") - 1
    after = lax.rem(section + 1, last + 1)
    before = lax.rem(section + last, last + 1)
    is_first = section == 0
    is_last = section == last
    place = lax.axis_index("dp")
    core = lax.rem(place, 2)
    z = lax.rem(place // 2, 4)
    y = place // 8
    partner = place + 1 - 2 * core
    y_peers = {a: place + 8 * (swap(y, a) - y) for a in (1, 3)}
    z_peers = {a: place + 2 * (swap(z, a) - z) for a in (1, 3)}
    early = jnp.logical_not(is_first)
    kind = (last - section) // last

    loads = [
        pltpu.make_async_copy(r.w_qkv_hbm.at[0, pl.ds(0, 768)], r.wqkv.at[pl.ds(0, 768)], r.load.at[0]),
        pltpu.make_async_copy(r.w_qkv_hbm.at[0, pl.ds(768, 256)], r.wqkv.at[pl.ds(768, 256)], r.load.at[1]),
        pltpu.make_async_copy(r.w_out_hbm.at[0], r.wout, r.load.at[6]),
    ]

    def entry(m):
        return pltpu.make_async_copy(r.patches.at[m, 0], r.xin.at[m], r.load.at[2 + m])

    def end_gradient(m):
        return pltpu.make_async_copy(r.cotangent.at[m, 0], r.gin.at[m], r.load.at[4 + m])

    def pass_on(m, i):
        c = pl.ds(CHUNKS[i].start, CHUNKS[i].stop - CHUNKS[i].start)
        return pltpu.make_async_remote_copy(
            src_ref=r.xout.at[m, :, c], dst_ref=r.acts.at[0, m, :, c],
            send_sem=r.x_send.at[m, i], recv_sem=r.x_recv.at[m, i],
            device_id={"section": after}, device_id_type=MESH,
        )

    def pass_back(m, i):
        c = pl.ds(CHUNKS[i].start, CHUNKS[i].stop - CHUNKS[i].start)
        return pltpu.make_async_remote_copy(
            src_ref=r.gout.at[m, :, c], dst_ref=r.gin.at[m, :, c],
            send_sem=r.g_send.at[m, i], recv_sem=r.g_recv.at[m, i],
            device_id={"section": before}, device_id_type=MESH,
        )

    def keep_output(m):
        return pltpu.make_async_copy(r.xout.at[m], r.outputs.at[0, m, 0], r.store.at[m])

    def keep_gradient(m):
        return pltpu.make_async_copy(r.gout.at[m], r.input_grads.at[0, m, 0], r.store.at[2 + m])

    def share(name, m, index):
        return pltpu.make_async_remote_copy(
            src_ref=getattr(r, name).at[m], dst_ref=getattr(r, "their_" + name).at[m],
            send_sem=r.share_send.at[index, m], recv_sem=r.share_recv.at[index, m],
            device_id={"dp": partner}, device_id_type=MESH,
        )

    shared = ["normed", "mixed", "gin", "gproj"]

    def axes(half):
        return ((y, y_peers), (z, z_peers)) if half == 0 else ((z, z_peers), (y, y_peers))

    def masks(j):
        return (1, 3) if j % 2 == 0 else (3, 1)

    def block(half, j, position):
        return r.part.at[0, j, position] if half == 0 else r.part.at[1, j, :, position]

    def send(half, j, step):
        (p, p_peers), (q, q_peers) = axes(half)
        a, b = masks(j)
        if step == 0:
            source, target, peer = block(half, j, swap(p, 2)), r.far_in, p_peers[a]
        elif step == 1:
            source, target, peer = block(half, j, swap(p, a)), r.near_in, p_peers[a]
        elif step == 2:
            source, target, peer = r.far_sum.at[half, j], r.last_in, p_peers[b]
        elif step == 3:
            source, target, peer = r.row.at[half, j, swap(q, 2)], r.row_far_in, q_peers[a]
        elif step == 4:
            source, target, peer = r.row.at[half, j, swap(q, a)], r.row_near_in, q_peers[a]
        else:
            source, target, peer = r.row_far_sum.at[half, j], r.row_last_in, q_peers[b]
        return pltpu.make_async_remote_copy(
            src_ref=source, dst_ref=target.at[half, j],
            send_sem=r.sum_send.at[half, j, step], recv_sem=r.sum_recv.at[half, j, step],
            device_id={"dp": peer}, device_id_type=MESH,
        )

    def sum_one(half, j):
        (p, _), _ = axes(half)
        send(half, j, 0).wait_recv()
        held = block(half, j, swap(p, masks(j)[1]))[...].astype(F32)
        r.far_sum[half, j] = (held + r.far_in[half, j].astype(F32)).astype(BF16)
        send(half, j, 2).start()

    def sum_two(half, j):
        (p, _), _ = axes(half)
        send(half, j, 1).wait_recv()
        send(half, j, 2).wait_recv()
        total = block(half, j, p)[...].astype(F32) + r.near_in[half, j].astype(F32)
        r.row[half, j] = (total + r.last_in[half, j].astype(F32)).astype(BF16)
        send(half, j, 3).start()
        send(half, j, 4).start()

    def sum_three(half, j):
        _, (q, _) = axes(half)
        send(half, j, 3).wait_recv()
        held = r.row[half, j, swap(q, masks(j)[1])].astype(F32)
        r.row_far_sum[half, j] = (held + r.row_far_in[half, j].astype(F32)).astype(BF16)
        send(half, j, 5).start()

    def sum_four(half, j):
        _, (q, _) = axes(half)
        send(half, j, 4).wait_recv()
        send(half, j, 5).wait_recv()
        total = r.row[half, j, q].astype(F32) + r.row_near_in[half, j].astype(F32)
        total = total + r.row_last_in[half, j].astype(F32)
        column = 2048 * half + 512 * j
        if column < 3072:
            r.total_qkv[0, :, column : column + 512] = total
        else:
            r.total_out_t[:, column - 3072 : column - 2560] = total

    @pl.when(is_first)
    def _():
        for m in range(2):
            entry(m).start()

    loads[0].start()

    @pl.when(is_last)
    def _():
        for m in range(2):
            end_gradient(m).start()

    barrier = pltpu.get_barrier_semaphore()
    for neighbour in (before, after):
        pl.semaphore_signal(barrier, inc=1, device_id={"section": neighbour}, device_id_type=MESH)
    for peer in [partner, *y_peers.values(), *z_peers.values()]:
        pl.semaphore_signal(barrier, inc=1, device_id={"dp": peer}, device_id_type=MESH)

    @pl.when(early)
    def _():
        for load in loads[1:]:
            load.start()
        for load in loads:
            load.wait()
        transpose_weights(r)

    def forward(m):
        @pl.when(is_first)
        def _():
            entry(m).wait()
            normalise(m, r)

        @pl.when(jnp.logical_not(is_first))
        def _():
            pass_on(m, 0).wait_recv()

        opening = jnp.logical_and(m == 0, jnp.logical_not(early))

        @pl.when(opening)
        def _():
            loads[0].wait()
            for load in loads[1:]:
                load.start()

        project_head(m, kind, r)

        @pl.when(jnp.logical_not(is_first))
        def _():
            pass_on(m, 1).wait_recv()

        @pl.when(opening)
        def _():
            r.columns[...] = jnp.zeros((16, 3072), F32)
            for load in loads[1:]:
                load.wait()

        attend(m, kind, r)
        project_out(m, r, HEAD)

        @pl.when(m == 0)
        def _():
            pl.semaphore_wait(barrier, 7)

        @pl.when(jnp.logical_not(is_last))
        def _():
            pass_on(m, 0).start()

        project_out(m, r, TAIL)

        @pl.when(jnp.logical_not(is_last))
        def _():
            pass_on(m, 1).start()

        keep_output(m).start()
        share("normed", m, 0).start()
        share("mixed", m, 1).start()

    def spread_normed():
        for m in range(2):
            share("normed", m, 0).wait_recv()
            share("mixed", m, 1).wait_recv()
        for m in range(2):
            spread(r, "normed_t", 128 * m, r.normed[m])
            spread(r, "normed_t", 256 + 128 * m, r.their_normed[m])

    def backward(m):
        @pl.when(jnp.logical_and(m == 0, jnp.logical_not(early)))
        def _():
            transpose_weights(r)

        @pl.when(jnp.logical_and(m == 0, is_first))
        def _():
            spread_normed()

        @pl.when(is_last)
        def _():
            end_gradient(m).wait()

        @pl.when(jnp.logical_not(is_last))
        def _():
            pass_back(m, 0).wait_recv()

        mixed_pull_head(m, r)

        @pl.when(jnp.logical_not(is_last))
        def _():
            pass_back(m, 1).wait_recv()

        share("gin", m, 2).start()
        attend_pull(m, r)
        share("gproj", m, 3).start()

        @pl.when(jnp.logical_not(is_first))
        def _():
            input_pull(m, r)
            pass_back(m, 0).start()
            pass_back(m, 1).start()
            keep_gradient(m).start()

    turns = section // last

    @pl.loop(0, 4)
    def _(t):
        back = turns * lax.rem(t, 2) + (1 - turns) * (t // 2)
        m = turns * (t // 2) + (1 - turns) * lax.rem(t, 2)

        @pl.when(back == 0)
        def _():
            forward(m)

        @pl.when(back == 1)
        def _():
            backward(m)

    @pl.when(jnp.logical_not(is_first))
    def _():
        spread_normed()

    for m in range(2):
        share("gproj", m, 3).wait_recv()

    def partial(half, j):
        column = 2048 * half + 512 * j
        if column < 3072:
            rows, name, c = r.normed_t, "gproj", slice(column, column + 512)
        else:
            rows, name, c = r.gin_t, "mixed", slice(column - 3072, column - 2560)
        rows = rows[:, core].reshape(512, 512)
        total = dg(rows[:, :256], getattr(r, name)[:, :, c].reshape(256, 512))
        total = total + dg(rows[:, 256:], getattr(r, "their_" + name)[:, :, c].reshape(256, 512))
        r.part[half, j] = total.astype(BF16).reshape(4, 4, 32, 512)

    pieces = [(half, j) for j in range(4) for half in range(2)]
    for half, j in pieces:
        if (half, j) == (1, 2):
            for m in range(2):
                share("gin", m, 2).wait_recv()
                spread(r, "gin_t", 128 * m, r.gin[m])
                spread(r, "gin_t", 256 + 128 * m, r.their_gin[m])
        partial(half, j)
        send(half, j, 0).start()
        send(half, j, 1).start()

    @pl.when(is_first)
    def _():
        @pl.loop(0, 2)
        def _(m):
            input_pull(m, r)
            keep_gradient(m).start()

    stages = (sum_one, sum_two, sum_three, sum_four)
    lags = (0, 3, 6, 9)
    for step in range(len(pieces) + lags[-1]):
        for lag, stage in zip(lags, stages):
            if 0 <= step - lag < len(pieces):
                stage(*pieces[step - lag])

    for half, j in pieces:
        for step in range(6):
            send(half, j, step).wait_send()
    for index, name in enumerate(shared):
        for m in range(2):
            share(name, m, index).wait_send()

    for m in range(2):
        keep_output(m).wait()
        keep_gradient(m).wait()

        @pl.when(jnp.logical_not(is_last))
        def _():
            pass_on(m, 0).wait_send()
            pass_on(m, 1).wait_send()

        @pl.when(jnp.logical_not(is_first))
        def _():
            pass_back(m, 0).wait_send()
            pass_back(m, 1).wait_send()


def relay(patches, segments, w_qkv, w_out, cotangent):
    inputs = [
        ("patches", patches, pl.ANY),
        ("segments", segments, pltpu.VMEM),
        ("w_qkv_hbm", w_qkv, pl.ANY),
        ("w_out_hbm", w_out, pl.ANY),
        ("cotangent", cotangent, pl.ANY),
    ]
    stacked = (1,) + patches.shape
    results = [
        ("outputs", stacked, BF16, pl.ANY),
        ("input_grads", stacked, BF16, pl.ANY),
        ("total_qkv", (1, 32, 3072), F32, pltpu.VMEM),
        ("total_out_t", (32, 1024), F32, pltpu.VMEM),
    ]
    block = (2, 128, 1024)
    scratch = [
        ("acts", pltpu.VMEM((2,) + block, BF16)),
        ("begun", pltpu.VMEM((128, 3072), F32)),
        ("columns", pltpu.VMEM((16, 3072), F32)),
        ("gin", pltpu.VMEM(block, BF16)),
        ("xout", pltpu.VMEM(block, BF16)),
        ("gout", pltpu.VMEM(block, BF16)),
        ("mixed", pltpu.VMEM(block, BF16)),
        ("their_normed", pltpu.VMEM(block, BF16)),
        ("their_mixed", pltpu.VMEM(block, BF16)),
        ("their_gin", pltpu.VMEM(block, BF16)),
        ("their_gproj", pltpu.VMEM((2, 128, 3072), BF16)),
        ("normed_t", pltpu.VMEM((16, 2, 32, 512), BF16)),
        ("gin_t", pltpu.VMEM((16, 2, 32, 512), BF16)),
        ("part", pltpu.VMEM((2, 4, 4, 4, 32, 512), BF16)),
        *((name, pltpu.VMEM((2, 4, 4, 32, 512), BF16)) for name in ("far_in", "near_in", "far_sum", "last_in", "row")),
        *((name, pltpu.VMEM((2, 4, 32, 512), BF16)) for name in ("row_far_in", "row_near_in", "row_far_sum", "row_last_in")),
        ("sum_send", pltpu.SemaphoreType.DMA((2, 4, 6))),
        ("sum_recv", pltpu.SemaphoreType.DMA((2, 4, 6))),
        ("share_send", pltpu.SemaphoreType.DMA((4, 2))),
        ("share_recv", pltpu.SemaphoreType.DMA((4, 2))),
        ("gproj", pltpu.VMEM((2, 128, 3072), BF16)),
        ("gn", pltpu.VMEM((128, 1024), F32)),
        ("wqkv", pltpu.VMEM((1024, 3072), BF16)),
        ("wout", pltpu.VMEM((1024, 1024), BF16)),
        ("wqkv_t", pltpu.VMEM((3072, 1024), BF16)),
        ("wout_t", pltpu.VMEM((1024, 1024), BF16)),
        ("xinv", pltpu.VMEM((2, 128, 128), F32)),
        ("qs", pltpu.VMEM((2, 8, 128, 128), BF16)),
        ("kt", pltpu.VMEM((2, 8, 128, 128), BF16)),
        ("v", pltpu.VMEM((2, 8, 128, 128), BF16)),
        ("qi", pltpu.VMEM((2, 8, 2, 128), F32)),
        ("ki", pltpu.VMEM((2, 8, 2, 128), F32)),
        ("probs", pltpu.VMEM((2, 8, 128, 256), BF16)),
        ("load", pltpu.SemaphoreType.DMA((7,))),
        ("store", pltpu.SemaphoreType.DMA((4,))),
        ("x_send", pltpu.SemaphoreType.DMA((2, 2))),
        ("x_recv", pltpu.SemaphoreType.DMA((2, 2))),
        ("g_send", pltpu.SemaphoreType.DMA((2, 2))),
        ("g_recv", pltpu.SemaphoreType.DMA((2, 2))),
    ]
    names = [i[0] for i in inputs] + [o[0] for o in results] + [s[0] for s in scratch]
    return pl.pallas_call(
        functools.partial(relay_kernel, names),
        out_shape=[jax.ShapeDtypeStruct(o[1], o[2]) for o in results],
        in_specs=[pl.BlockSpec(memory_space=i[2]) for i in inputs],
        out_specs=[pl.BlockSpec(memory_space=o[3]) for o in results],
        scratch_shapes=[s[1] for s in scratch],
        compiler_params=pltpu.CompilerParams(
            collective_id=0, has_side_effects=True, vmem_limit_bytes=58 << 20
        ),
        name="relay",
    )(*[i[1] for i in inputs])


def settle_kernel(count, *refs):
    sources, targets, held = refs[:count], refs[count : 2 * count], refs[2 * count : 3 * count]
    read, written = refs[-2:]
    into = [pltpu.make_async_copy(a, b, read.at[i]) for i, (a, b) in enumerate(zip(sources, held))]
    out = [pltpu.make_async_copy(a, b, written.at[i]) for i, (a, b) in enumerate(zip(held, targets))]
    for copy in into:
        copy.start()
    for first, second in zip(into, out):
        first.wait()
        second.start()
    for copy in out:
        copy.wait()


def settle(arrays):
    return pl.pallas_call(
        functools.partial(settle_kernel, len(arrays)),
        out_shape=[jax.ShapeDtypeStruct(a.shape, a.dtype) for a in arrays],
        in_specs=[pl.BlockSpec(memory_space=pl.ANY)] * len(arrays),
        out_specs=[pl.BlockSpec(memory_space=pl.ANY)] * len(arrays),
        scratch_shapes=[pltpu.VMEM(a.shape, a.dtype) for a in arrays]
        + [pltpu.SemaphoreType.DMA((len(arrays),))] * 2,
        name="settle",
    )(*arrays)


def on_device(patches, segment_ids, weights_qkv, weights_out, cotangent):
    produced, grads, total_qkv, total_out_t = settle(
        relay(patches, segment_ids, weights_qkv, weights_out, cotangent)
    )
    return (produced, grads, total_qkv, total_out_t.T[None])


def solution(mesh):
    return jax.shard_map(
        on_device,
        mesh=mesh,
        in_specs=(
            P(None, "dp", None, None),
            P(None, "dp", None),
            P("section", None, None),
            P("section", None, None),
            P(None, "dp", None, None),
        ),
        out_specs=(
            P("section", None, "dp", None, None),
            P("section", None, "dp", None, None),
            P("section", "dp", None),
            P("section", None, "dp"),
        ),
        check_vma=False,
    )
```

```python
import functools
import types

import jax
import jax.numpy as jnp
from jax import lax
from jax.experimental import pallas as pl
from jax.experimental.pallas import tpu as pltpu
from jax.sharding import PartitionSpec as P

BF16 = jnp.bfloat16
F32 = jnp.float32
EPSILON = 1e-6
MESH = pl.DeviceIdType.MESH
CHUNKS = (slice(0, 768), slice(768, 1024))
HEAD, TAIL = CHUNKS


def dg(a,b,ca=1,cb=0): return lax.dot_general(a,b,(((ca,),(cb,)),((),())),preferred_element_type=F32)

def block_diagonal(pair):
    blank = jnp.zeros((64, pair.shape[1]), pair.dtype)
    top = jnp.concatenate([pair[:64], blank], axis=1)
    bottom = jnp.concatenate([blank, pair[64:]], axis=1)
    return jnp.concatenate([top, bottom], axis=0)

def block_diagonal_rows(pair):
    left = lax.broadcasted_iota(jnp.int32, pair.shape, 1) < 64
    blank = jnp.zeros_like(pair)
    return jnp.concatenate([jnp.where(left, pair, blank), jnp.where(left, blank, pair)], axis=0)


def head_norm(rows):
    grouped = rows.reshape(2, 64, rows.shape[1])
    centred = grouped - jnp.mean(grouped, axis=1, keepdims=True)
    inverse = lax.rsqrt(jnp.mean(centred * centred, axis=1, keepdims=True) + EPSILON)
    return (centred * inverse).reshape(rows.shape), inverse[:, 0, :]

def head_norm_pull(grad, normed, inverse):
    tokens = grad.shape[1]
    g = grad.reshape(2, 64, tokens)
    n = normed.reshape(2, 64, tokens)
    first = jnp.mean(g, axis=1, keepdims=True)
    second = jnp.mean(g * n, axis=1, keepdims=True)
    return ((g - first - n * second) * inverse[:, None, :]).reshape(grad.shape)

def normalise(m, r):
    x = r.xin[m].astype(F32)
    average = jnp.mean(x, axis=-1, keepdims=True)
    centred = x - average
    inverse = lax.rsqrt(jnp.mean(centred * centred, axis=-1, keepdims=True) + EPSILON)
    r.xinv[m] = jnp.broadcast_to(inverse, (128, 128))
    r.normed[m] = (centred * inverse).astype(BF16)
    return average, inverse


def project_head(m, kind, r):
    for j in range(6):
        c = slice(512 * j, 512 * j + 512)
        r.begun[:, c] = dg(r.acts[kind, m, :, HEAD], r.wqkv[HEAD, c])


def attend(m, kind, r):
    queries_in = jnp.broadcast_to(r.segments[m].astype(F32), (128, 128))
    allowed = queries_in == queries_in.T
    allowed = jnp.concatenate([allowed, allowed], axis=1)
    rest = r.acts[kind, m, :, TAIL]
    raw = 1.0 - kind.astype(F32)
    average, inverse = normalise(m, r)
    average = average * raw
    inverse = inverse * raw + (1.0 - raw)
    live = {}

    def project(quad):
        for name, start in (("q", 0), ("k", 1024), ("v", 2048)):
            column = start + 256 * quad
            c = slice(column, column + 256)
            product = r.begun[:, c] + dg(rest, r.wqkv[TAIL, c])
            live[name, quad] = (product - average * r.columns[:1, c]) * inverse

    def norms(quad):
        for half in range(2):
            pair = 2 * quad + half
            c = slice(128 * half, 128 * half + 128)
            q, r.qi[m, pair] = head_norm(live["q", quad][:, c].T)
            k, r.ki[m, pair] = head_norm(live["k", quad][:, c].T)
            v = live["v", quad][:, c].astype(BF16)
            qs, kt = (q * 0.125).astype(BF16), k.astype(BF16)
            r.qs[m, pair], r.kt[m, pair], r.v[m, pair] = qs, kt, v
            live["qs", pair], live["kn", pair], live["vt", pair] = qs, kt.T, v.T

    def scores(quad):
        for pair in (2 * quad, 2 * quad + 1):
            live["s", pair] = dg(live["kn", pair], block_diagonal(live["qs", pair]))

    def softmax(quad):
        for pair in (2 * quad, 2 * quad + 1):
            w = jnp.where(allowed, jnp.exp(live["s", pair]), 0.0)
            p = (w * (1.0 / jnp.sum(w, axis=0, keepdims=True))).astype(BF16)
            r.probs[m, pair] = p
            live["p", pair] = p

    def mix(quad):
        for pair in (2 * quad, 2 * quad + 1):
            vt, p = live["vt", pair], live["p", pair]
            o = [dg(vt[64 * i : 64 * i + 64], p[:, 128 * i : 128 * i + 128]) for i in range(2)]
            live["o", pair] = jnp.concatenate(o, axis=0).astype(BF16)

    def turn(quad):
        for pair in (2 * quad, 2 * quad + 1):
            r.mixed[m, :, 128 * pair : 128 * pair + 128] = live["o", pair].T

    for stage in (project, norms, scores, softmax, mix, turn):
        for quad in range(4):
            stage(quad)


def project_out(m, r, chunk):
    mixed = r.mixed[m]
    for start in range(chunk.start, chunk.stop, 256):
        c = slice(start, start + 256)
        branch = dg(mixed, r.wout[:, c])
        r.xout[m, :, c] = (r.xin[m, :, c].astype(F32) + branch).astype(BF16)


def mixed_pull_head(m, r):
    for j in range(4):
        c = slice(256 * j, 256 * j + 256)
        r.gn[:, c] = dg(r.gin[m, :, HEAD], r.wout_t[HEAD, c])


def attend_pull(m, r):
    rest = r.gin[m, :, TAIL]
    live = {}

    def project(quad):
        c = slice(256 * quad, 256 * quad + 256)
        go4 = (r.gn[:, c] + dg(rest, r.wout_t[TAIL, c])).astype(BF16)
        for half in range(2):
            go = go4[:, 128 * half : 128 * half + 128]
            live["rows", 2 * quad + half], live["go", 2 * quad + half] = go, go.T

    def probs_pull(quad):
        for pair in (2 * quad, 2 * quad + 1):
            live["dp", pair] = dg(r.v[m, pair], block_diagonal(live["go", pair]))

    def values_pull(quad):
        for pair in (2 * quad, 2 * quad + 1):
            gv = dg(r.probs[m, pair], block_diagonal_rows(live["rows", pair]))
            r.gproj[m, :, 2048 + 128 * pair : 2176 + 128 * pair] = gv.astype(BF16)

    def scores_pull(quad):
        for pair in (2 * quad, 2 * quad + 1):
            p = r.probs[m, pair].astype(F32)
            pd = p * live["dp", pair]
            live["ds", pair] = (pd - p * jnp.sum(pd, axis=0, keepdims=True)).astype(BF16)

    def heads_pull(quad):
        for pair in (2 * quad, 2 * quad + 1):
            ds, kt, qs = live["ds", pair], r.kt[m, pair], r.qs[m, pair]
            cut = [(slice(64 * i, 64 * i + 64), slice(128 * i, 128 * i + 128)) for i in range(2)]
            live["gq", pair] = jnp.concatenate([dg(kt[i], ds[:, c]) for i, c in cut], axis=0)
            live["gk", pair] = dg(ds, block_diagonal_rows(qs.T)).T

    def norms_pull(quad):
        for pair in (2 * quad, 2 * quad + 1):
            qs, kt = r.qs[m, pair].astype(F32), r.kt[m, pair].astype(F32)
            gq = head_norm_pull(live["gq", pair] * 0.125, qs * 8.0, r.qi[m, pair])
            gk = head_norm_pull(live["gk", pair], kt, r.ki[m, pair])
            live["gq", pair], live["gk", pair] = gq.astype(BF16), gk.astype(BF16)

    def turn(quad):
        for pair in (2 * quad, 2 * quad + 1):
            for name, start in (("gq", 0), ("gk", 1024)):
                column = start + 128 * pair
                r.gproj[m, :, column : column + 128] = live[name, pair].T

    for stage in (project, probs_pull, scores_pull, values_pull, heads_pull, norms_pull, turn):
        for quad in range(4):
            stage(quad)


def input_pull(m, r):
    gproj = r.gproj[m]
    for j in range(4):
        r.gn[:, 256*j:256*j+256] = dg(gproj, r.wqkv_t[:, 256*j:256*j+256])
    gn = r.gn[...]
    n = r.normed[m].astype(F32)
    first = jnp.mean(gn, axis=-1, keepdims=True)
    second = jnp.mean(gn * n, axis=-1, keepdims=True)
    dx = (gn - first - n * second) * r.xinv[m][:, :1]
    r.gout[m] = (r.gin[m].astype(F32) + dx).astype(BF16)

def transpose_weights(r):
    for j in range(8):
        r.wqkv_t[:, 128*j:128*j+128] = r.wqkv[128*j:128*j+128, :].T
        r.wout_t[:, 128*j:128*j+128] = r.wout[128*j:128*j+128, :].T
    for j in range(6):
        c = slice(512 * j, 512 * j + 512)
        r.columns[:, c] = dg(jnp.ones((16, 1024), BF16), r.wqkv[:, c])


def spread(r, name, column, rows):
    getattr(r, name)[:, :, :, column : column + 128] = rows.T.reshape(16, 2, 32, 128)


def swap(p, mask):
    if mask == 1:
        return p + 1 - 2 * lax.rem(p, 2)
    if mask == 2:
        return lax.rem(p + 2, 4)
    return 3 - p


def relay_kernel(names, *refs):
    r = types.SimpleNamespace(**dict(zip(names, refs)))
    r.xin, r.normed = r.acts.at[0], r.acts.at[1]
    section = lax.axis_index("section")
    last = lax.axis_size("section") - 1
    after = lax.rem(section + 1, last + 1)
    before = lax.rem(section + last, last + 1)
    is_first = section == 0
    is_last = section == last
    place = lax.axis_index("dp")
    core = lax.rem(place, 2)
    z = lax.rem(place // 2, 4)
    y = place // 8
    partner = place + 1 - 2 * core
    y_peers = {a: place + 8 * (swap(y, a) - y) for a in (1, 2, 3)}
    z_peers = {a: place + 2 * (swap(z, a) - z) for a in (1, 2, 3)}
    early = jnp.logical_not(is_first)
    kind = (last - section) // last

    loads = [
        pltpu.make_async_copy(r.w_qkv_hbm.at[0, pl.ds(0, 768)], r.wqkv.at[pl.ds(0, 768)], r.load.at[0]),
        pltpu.make_async_copy(r.w_qkv_hbm.at[0, pl.ds(768, 256)], r.wqkv.at[pl.ds(768, 256)], r.load.at[1]),
        pltpu.make_async_copy(r.w_out_hbm.at[0], r.wout, r.load.at[6]),
    ]

    def entry(m):
        return pltpu.make_async_copy(r.patches.at[m, 0], r.xin.at[m], r.load.at[2 + m])

    def end_gradient(m):
        return pltpu.make_async_copy(r.cotangent.at[m, 0], r.gin.at[m], r.load.at[4 + m])

    def pass_on(m, i):
        c = pl.ds(CHUNKS[i].start, CHUNKS[i].stop - CHUNKS[i].start)
        return pltpu.make_async_remote_copy(
            src_ref=r.xout.at[m, :, c], dst_ref=r.acts.at[0, m, :, c],
            send_sem=r.x_send.at[m, i], recv_sem=r.x_recv.at[m, i],
            device_id={"section": after}, device_id_type=MESH,
        )

    def pass_back(m, i):
        c = pl.ds(CHUNKS[i].start, CHUNKS[i].stop - CHUNKS[i].start)
        return pltpu.make_async_remote_copy(
            src_ref=r.gout.at[m, :, c], dst_ref=r.gin.at[m, :, c],
            send_sem=r.g_send.at[m, i], recv_sem=r.g_recv.at[m, i],
            device_id={"section": before}, device_id_type=MESH,
        )

    def keep_output(m):
        return pltpu.make_async_copy(r.xout.at[m], r.outputs.at[0, m, 0], r.store.at[m])

    def keep_gradient(m):
        return pltpu.make_async_copy(r.gout.at[m], r.input_grads.at[0, m, 0], r.store.at[2 + m])

    def share(name, m, index):
        return pltpu.make_async_remote_copy(
            src_ref=getattr(r, name).at[m], dst_ref=getattr(r, "their_" + name).at[m],
            send_sem=r.share_send.at[index, m], recv_sem=r.share_recv.at[index, m],
            device_id={"dp": partner}, device_id_type=MESH,
        )

    shared = ["normed", "mixed", "gin", "gproj"]

    def axes(half):
        return ((y, y_peers), (z, z_peers)) if half == 0 else ((z, z_peers), (y, y_peers))

    def masks(j):
        return (1, 3) if j % 2 == 0 else (3, 1)

    def block(half, j, position):
        return r.part.at[0, j, position] if half == 0 else r.part.at[1, j, :, position]

    def send(half, j, step):
        (p, p_peers), (q, q_peers) = axes(half)
        a, b = masks(j)
        if step == 0:
            source, target, peer = block(half, j, swap(p, 2)), r.far_in, p_peers[a]
        elif step == 1:
            source, target, peer = block(half, j, swap(p, a)), r.near_in, p_peers[a]
        elif step == 2:
            source, target, peer = r.far_sum.at[half, j], r.last_in, p_peers[b]
        else:
            a = step - 2
            source, target, peer = r.row.at[half, j, swap(q, a)], r.row_in.at[a - 1], q_peers[a]
        return pltpu.make_async_remote_copy(
            src_ref=source, dst_ref=target.at[half, j],
            send_sem=r.sum_send.at[half, j, step], recv_sem=r.sum_recv.at[half, j, step],
            device_id={"dp": peer}, device_id_type=MESH,
        )

    def sum_one(half, j):
        (p, _), _ = axes(half)
        send(half, j, 0).wait_recv()
        held = block(half, j, swap(p, masks(j)[1]))[...].astype(F32)
        r.far_sum[half, j] = (held + r.far_in[half, j].astype(F32)).astype(BF16)
        send(half, j, 2).start()

    def sum_two(half, j):
        (p, _), _ = axes(half)
        send(half, j, 1).wait_recv()
        send(half, j, 2).wait_recv()
        total = block(half, j, p)[...].astype(F32) + r.near_in[half, j].astype(F32)
        r.row[half, j] = (total + r.last_in[half, j].astype(F32)).astype(BF16)
        for step in (3, 4, 5):
            send(half, j, step).start()

    def sum_three(half, j):
        _, (q, _) = axes(half)
        total = r.row[half, j, q].astype(F32)
        for step in (3, 4, 5):
            send(half, j, step).wait_recv()
        for k in range(3):
            total = total + r.row_in[k, half, j].astype(F32)
        column = 2048 * half + 512 * j
        if column < 3072:
            r.total_qkv[0, :, column : column + 512] = total
        else:
            r.total_out_t[:, column - 3072 : column - 2560] = total

    @pl.when(is_first)
    def _():
        for m in range(2):
            entry(m).start()

    loads[0].start()

    @pl.when(is_last)
    def _():
        for m in range(2):
            end_gradient(m).start()

    barrier = pltpu.get_barrier_semaphore()
    for neighbour in (before, after):
        pl.semaphore_signal(barrier, inc=1, device_id={"section": neighbour}, device_id_type=MESH)
    for peer in [partner, *y_peers.values(), *z_peers.values()]:
        pl.semaphore_signal(barrier, inc=1, device_id={"dp": peer}, device_id_type=MESH)

    @pl.when(early)
    def _():
        for load in loads[1:]:
            load.start()
        for load in loads:
            load.wait()
        transpose_weights(r)

    def forward(m):
        @pl.when(is_first)
        def _():
            entry(m).wait()
            normalise(m, r)

        @pl.when(jnp.logical_not(is_first))
        def _():
            pass_on(m, 0).wait_recv()

        opening = jnp.logical_and(m == 0, jnp.logical_not(early))

        @pl.when(opening)
        def _():
            loads[0].wait()
            for load in loads[1:]:
                load.start()

        project_head(m, kind, r)

        @pl.when(jnp.logical_not(is_first))
        def _():
            pass_on(m, 1).wait_recv()

        @pl.when(opening)
        def _():
            r.columns[...] = jnp.zeros((16, 3072), F32)
            for load in loads[1:]:
                load.wait()

        attend(m, kind, r)
        project_out(m, r, HEAD)

        @pl.when(m == 0)
        def _():
            pl.semaphore_wait(barrier, 9)

        @pl.when(jnp.logical_not(is_last))
        def _():
            pass_on(m, 0).start()

        project_out(m, r, TAIL)

        @pl.when(jnp.logical_not(is_last))
        def _():
            pass_on(m, 1).start()

        keep_output(m).start()
        share("normed", m, 0).start()
        share("mixed", m, 1).start()

    def spread_normed():
        for m in range(2):
            share("normed", m, 0).wait_recv()
            share("mixed", m, 1).wait_recv()
        for m in range(2):
            spread(r, "normed_t", 128 * m, r.normed[m])
            spread(r, "normed_t", 256 + 128 * m, r.their_normed[m])

    def backward(m):
        @pl.when(jnp.logical_and(m == 0, jnp.logical_not(early)))
        def _():
            transpose_weights(r)

        @pl.when(jnp.logical_and(m == 0, is_first))
        def _():
            spread_normed()

        @pl.when(is_last)
        def _():
            end_gradient(m).wait()

        @pl.when(jnp.logical_not(is_last))
        def _():
            pass_back(m, 0).wait_recv()

        mixed_pull_head(m, r)

        @pl.when(jnp.logical_not(is_last))
        def _():
            pass_back(m, 1).wait_recv()

        share("gin", m, 2).start()
        attend_pull(m, r)
        share("gproj", m, 3).start()

        @pl.when(jnp.logical_not(is_first))
        def _():
            input_pull(m, r)
            pass_back(m, 0).start()
            pass_back(m, 1).start()
            keep_gradient(m).start()

    turns = section // last

    @pl.loop(0, 4)
    def _(t):
        back = turns * lax.rem(t, 2) + (1 - turns) * (t // 2)
        m = turns * (t // 2) + (1 - turns) * lax.rem(t, 2)

        @pl.when(back == 0)
        def _():
            forward(m)

        @pl.when(back == 1)
        def _():
            backward(m)

    @pl.when(jnp.logical_not(is_first))
    def _():
        spread_normed()

    for m in range(2):
        share("gproj", m, 3).wait_recv()

    def partial(half, j):
        column = 2048 * half + 512 * j
        if column < 3072:
            rows, name, c = r.normed_t, "gproj", slice(column, column + 512)
        else:
            rows, name, c = r.gin_t, "mixed", slice(column - 3072, column - 2560)
        rows = rows[:, core].reshape(512, 512)
        total = dg(rows[:, :256], getattr(r, name)[:, :, c].reshape(256, 512))
        total = total + dg(rows[:, 256:], getattr(r, "their_" + name)[:, :, c].reshape(256, 512))
        r.part[half, j] = total.astype(BF16).reshape(4, 4, 32, 512)

    pieces = [(half, j) for j in range(4) for half in range(2)]
    for half, j in pieces:
        if (half, j) == (1, 2):
            for m in range(2):
                share("gin", m, 2).wait_recv()
                spread(r, "gin_t", 128 * m, r.gin[m])
                spread(r, "gin_t", 256 + 128 * m, r.their_gin[m])
        partial(half, j)
        send(half, j, 0).start()
        send(half, j, 1).start()

    @pl.when(is_first)
    def _():
        @pl.loop(0, 2)
        def _(m):
            input_pull(m, r)
            keep_gradient(m).start()

    stages = (sum_one, sum_two, sum_three)
    lags = (0, 3, 6)
    for step in range(len(pieces) + lags[-1]):
        for lag, stage in zip(lags, stages):
            if 0 <= step - lag < len(pieces):
                stage(*pieces[step - lag])

    for half, j in pieces:
        for step in range(6):
            send(half, j, step).wait_send()
    for index, name in enumerate(shared):
        for m in range(2):
            share(name, m, index).wait_send()

    for m in range(2):
        keep_output(m).wait()
        keep_gradient(m).wait()

        @pl.when(jnp.logical_not(is_last))
        def _():
            pass_on(m, 0).wait_send()
            pass_on(m, 1).wait_send()

        @pl.when(jnp.logical_not(is_first))
        def _():
            pass_back(m, 0).wait_send()
            pass_back(m, 1).wait_send()


def relay(patches, segments, w_qkv, w_out, cotangent):
    inputs = [
        ("patches", patches, pl.ANY),
        ("segments", segments, pltpu.VMEM),
        ("w_qkv_hbm", w_qkv, pl.ANY),
        ("w_out_hbm", w_out, pl.ANY),
        ("cotangent", cotangent, pl.ANY),
    ]
    stacked = (1,) + patches.shape
    results = [
        ("outputs", stacked, BF16, pl.ANY),
        ("input_grads", stacked, BF16, pl.ANY),
        ("total_qkv", (1, 32, 3072), F32, pltpu.VMEM),
        ("total_out_t", (32, 1024), F32, pltpu.VMEM),
    ]
    block = (2, 128, 1024)
    scratch = [
        ("acts", pltpu.VMEM((2,) + block, BF16)),
        ("begun", pltpu.VMEM((128, 3072), F32)),
        ("columns", pltpu.VMEM((16, 3072), F32)),
        ("gin", pltpu.VMEM(block, BF16)),
        ("xout", pltpu.VMEM(block, BF16)),
        ("gout", pltpu.VMEM(block, BF16)),
        ("mixed", pltpu.VMEM(block, BF16)),
        ("their_normed", pltpu.VMEM(block, BF16)),
        ("their_mixed", pltpu.VMEM(block, BF16)),
        ("their_gin", pltpu.VMEM(block, BF16)),
        ("their_gproj", pltpu.VMEM((2, 128, 3072), BF16)),
        ("normed_t", pltpu.VMEM((16, 2, 32, 512), BF16)),
        ("gin_t", pltpu.VMEM((16, 2, 32, 512), BF16)),
        ("part", pltpu.VMEM((2, 4, 4, 4, 32, 512), BF16)),
        *((name, pltpu.VMEM((2, 4, 4, 32, 512), BF16)) for name in ("far_in", "near_in", "far_sum", "last_in", "row")),
        ("row_in", pltpu.VMEM((3, 2, 4, 32, 512), BF16)),
        ("sum_send", pltpu.SemaphoreType.DMA((2, 4, 6))),
        ("sum_recv", pltpu.SemaphoreType.DMA((2, 4, 6))),
        ("share_send", pltpu.SemaphoreType.DMA((4, 2))),
        ("share_recv", pltpu.SemaphoreType.DMA((4, 2))),
        ("gproj", pltpu.VMEM((2, 128, 3072), BF16)),
        ("gn", pltpu.VMEM((128, 1024), F32)),
        ("wqkv", pltpu.VMEM((1024, 3072), BF16)),
        ("wout", pltpu.VMEM((1024, 1024), BF16)),
        ("wqkv_t", pltpu.VMEM((3072, 1024), BF16)),
        ("wout_t", pltpu.VMEM((1024, 1024), BF16)),
        ("xinv", pltpu.VMEM((2, 128, 128), F32)),
        ("qs", pltpu.VMEM((2, 8, 128, 128), BF16)),
        ("kt", pltpu.VMEM((2, 8, 128, 128), BF16)),
        ("v", pltpu.VMEM((2, 8, 128, 128), BF16)),
        ("qi", pltpu.VMEM((2, 8, 2, 128), F32)),
        ("ki", pltpu.VMEM((2, 8, 2, 128), F32)),
        ("probs", pltpu.VMEM((2, 8, 128, 256), BF16)),
        ("load", pltpu.SemaphoreType.DMA((7,))),
        ("store", pltpu.SemaphoreType.DMA((4,))),
        ("x_send", pltpu.SemaphoreType.DMA((2, 2))),
        ("x_recv", pltpu.SemaphoreType.DMA((2, 2))),
        ("g_send", pltpu.SemaphoreType.DMA((2, 2))),
        ("g_recv", pltpu.SemaphoreType.DMA((2, 2))),
    ]
    names = [i[0] for i in inputs] + [o[0] for o in results] + [s[0] for s in scratch]
    return pl.pallas_call(
        functools.partial(relay_kernel, names),
        out_shape=[jax.ShapeDtypeStruct(o[1], o[2]) for o in results],
        in_specs=[pl.BlockSpec(memory_space=i[2]) for i in inputs],
        out_specs=[pl.BlockSpec(memory_space=o[3]) for o in results],
        scratch_shapes=[s[1] for s in scratch],
        compiler_params=pltpu.CompilerParams(
            collective_id=0, has_side_effects=True, vmem_limit_bytes=58 << 20
        ),
        name="relay",
    )(*[i[1] for i in inputs])


def settle_kernel(count, *refs):
    sources, targets, held = refs[:count], refs[count : 2 * count], refs[2 * count : 3 * count]
    read, written = refs[-2:]
    into = [pltpu.make_async_copy(a, b, read.at[i]) for i, (a, b) in enumerate(zip(sources, held))]
    out = [pltpu.make_async_copy(a, b, written.at[i]) for i, (a, b) in enumerate(zip(held, targets))]
    for copy in into:
        copy.start()
    for first, second in zip(into, out):
        first.wait()
        second.start()
    for copy in out:
        copy.wait()


def settle(arrays):
    return pl.pallas_call(
        functools.partial(settle_kernel, len(arrays)),
        out_shape=[jax.ShapeDtypeStruct(a.shape, a.dtype) for a in arrays],
        in_specs=[pl.BlockSpec(memory_space=pl.ANY)] * len(arrays),
        out_specs=[pl.BlockSpec(memory_space=pl.ANY)] * len(arrays),
        scratch_shapes=[pltpu.VMEM(a.shape, a.dtype) for a in arrays]
        + [pltpu.SemaphoreType.DMA((len(arrays),))] * 2,
        name="settle",
    )(*arrays)


def on_device(patches, segment_ids, weights_qkv, weights_out, cotangent):
    produced, grads, total_qkv, total_out_t = settle(
        relay(patches, segment_ids, weights_qkv, weights_out, cotangent)
    )
    return (produced, grads, total_qkv, total_out_t.T[None])


def solution(mesh):
    return jax.shard_map(
        on_device,
        mesh=mesh,
        in_specs=(
            P(None, "dp", None, None),
            P(None, "dp", None),
            P("section", None, None),
            P("section", None, None),
            P(None, "dp", None, None),
        ),
        out_specs=(
            P("section", None, "dp", None, None),
            P("section", None, "dp", None, None),
            P("section", "dp", None),
            P("section", None, "dp"),
        ),
        check_vma=False,
    )
```

```python
import functools
import types

import jax
import jax.numpy as jnp
from jax import lax
from jax.experimental import pallas as pl
from jax.experimental.pallas import tpu as pltpu
from jax.sharding import PartitionSpec as P

BF16 = jnp.bfloat16
F32 = jnp.float32
EPSILON = 1e-6
MESH = pl.DeviceIdType.MESH
CHUNKS = (slice(0, 768), slice(768, 1024))
HEAD, TAIL = CHUNKS


def dg(a,b,ca=1,cb=0): return lax.dot_general(a,b,(((ca,),(cb,)),((),())),preferred_element_type=F32)

def block_diagonal(pair):
    blank = jnp.zeros((64, pair.shape[1]), pair.dtype)
    top = jnp.concatenate([pair[:64], blank], axis=1)
    bottom = jnp.concatenate([blank, pair[64:]], axis=1)
    return jnp.concatenate([top, bottom], axis=0)

def block_diagonal_rows(pair):
    left = lax.broadcasted_iota(jnp.int32, pair.shape, 1) < 64
    blank = jnp.zeros_like(pair)
    return jnp.concatenate([jnp.where(left, pair, blank), jnp.where(left, blank, pair)], axis=0)


def head_norm(rows):
    grouped = rows.reshape(2, 64, rows.shape[1])
    centred = grouped - jnp.mean(grouped, axis=1, keepdims=True)
    inverse = lax.rsqrt(jnp.mean(centred * centred, axis=1, keepdims=True) + EPSILON)
    return (centred * inverse).reshape(rows.shape), inverse[:, 0, :]

def head_norm_pull(grad, normed, inverse):
    tokens = grad.shape[1]
    g = grad.reshape(2, 64, tokens)
    n = normed.reshape(2, 64, tokens)
    first = jnp.mean(g, axis=1, keepdims=True)
    second = jnp.mean(g * n, axis=1, keepdims=True)
    return ((g - first - n * second) * inverse[:, None, :]).reshape(grad.shape)

def normalise(m, r):
    x = r.xin[m].astype(F32)
    average = jnp.mean(x, axis=-1, keepdims=True)
    centred = x - average
    inverse = lax.rsqrt(jnp.mean(centred * centred, axis=-1, keepdims=True) + EPSILON)
    r.xinv[m] = jnp.broadcast_to(inverse, (128, 128))
    r.normed[m] = (centred * inverse).astype(BF16)
    return average, inverse


def project_head(m, kind, r):
    for j in range(6):
        c = slice(512 * j, 512 * j + 512)
        r.begun[:, c] = dg(r.acts[kind, m, :, HEAD], r.wqkv[HEAD, c])


def attend(m, kind, r):
    queries_in = jnp.broadcast_to(r.segments[m].astype(F32), (128, 128))
    allowed = queries_in == queries_in.T
    allowed = jnp.concatenate([allowed, allowed], axis=1)
    rest = r.acts[kind, m, :, TAIL]
    raw = 1.0 - kind.astype(F32)
    average, inverse = normalise(m, r)
    average = average * raw
    inverse = inverse * raw + (1.0 - raw)
    live = {}

    def project(quad):
        for name, start in (("q", 0), ("k", 1024), ("v", 2048)):
            column = start + 256 * quad
            c = slice(column, column + 256)
            product = r.begun[:, c] + dg(rest, r.wqkv[TAIL, c])
            live[name, quad] = (product - average * r.columns[:1, c]) * inverse

    def norms(quad):
        for half in range(2):
            pair = 2 * quad + half
            c = slice(128 * half, 128 * half + 128)
            q, r.qi[m, pair] = head_norm(live["q", quad][:, c].T)
            k, r.ki[m, pair] = head_norm(live["k", quad][:, c].T)
            v = live["v", quad][:, c].astype(BF16)
            qs, kt = (q * 0.125).astype(BF16), k.astype(BF16)
            r.qs[m, pair], r.kt[m, pair], r.v[m, pair] = qs, kt, v
            live["qs", pair], live["kn", pair], live["vt", pair] = qs, kt.T, v.T

    def scores(quad):
        for pair in (2 * quad, 2 * quad + 1):
            live["s", pair] = dg(live["kn", pair], block_diagonal(live["qs", pair]))

    def softmax(quad):
        for pair in (2 * quad, 2 * quad + 1):
            w = jnp.where(allowed, jnp.exp(live["s", pair]), 0.0)
            p = (w * (1.0 / jnp.sum(w, axis=0, keepdims=True))).astype(BF16)
            r.probs[m, pair] = p
            live["p", pair] = p

    def mix(quad):
        for pair in (2 * quad, 2 * quad + 1):
            vt, p = live["vt", pair], live["p", pair]
            o = [dg(vt[64 * i : 64 * i + 64], p[:, 128 * i : 128 * i + 128]) for i in range(2)]
            live["o", pair] = jnp.concatenate(o, axis=0).astype(BF16)

    def turn(quad):
        for pair in (2 * quad, 2 * quad + 1):
            r.mixed[m, :, 128 * pair : 128 * pair + 128] = live["o", pair].T

    for stage in (project, norms, scores, softmax, mix, turn):
        for quad in range(4):
            stage(quad)


def project_out(m, r, chunk):
    mixed = r.mixed[m]
    for start in range(chunk.start, chunk.stop, 256):
        c = slice(start, start + 256)
        branch = dg(mixed, r.wout[:, c])
        r.xout[m, :, c] = (r.xin[m, :, c].astype(F32) + branch).astype(BF16)


def mixed_pull_head(m, r):
    for j in range(4):
        c = slice(256 * j, 256 * j + 256)
        r.gn[:, c] = dg(r.gin[m, :, HEAD], r.wout_t[HEAD, c])


def attend_pull(m, r):
    rest = r.gin[m, :, TAIL]
    live = {}

    def project(quad):
        c = slice(256 * quad, 256 * quad + 256)
        go4 = (r.gn[:, c] + dg(rest, r.wout_t[TAIL, c])).astype(BF16)
        for half in range(2):
            go = go4[:, 128 * half : 128 * half + 128]
            live["rows", 2 * quad + half], live["go", 2 * quad + half] = go, go.T

    def probs_pull(quad):
        for pair in (2 * quad, 2 * quad + 1):
            live["dp", pair] = dg(r.v[m, pair], block_diagonal(live["go", pair]))

    def values_pull(quad):
        for pair in (2 * quad, 2 * quad + 1):
            gv = dg(r.probs[m, pair], block_diagonal_rows(live["rows", pair]))
            r.gproj[m, :, 2048 + 128 * pair : 2176 + 128 * pair] = gv.astype(BF16)

    def scores_pull(quad):
        for pair in (2 * quad, 2 * quad + 1):
            p = r.probs[m, pair].astype(F32)
            pd = p * live["dp", pair]
            live["ds", pair] = (pd - p * jnp.sum(pd, axis=0, keepdims=True)).astype(BF16)

    def heads_pull(quad):
        for pair in (2 * quad, 2 * quad + 1):
            ds, kt, qs = live["ds", pair], r.kt[m, pair], r.qs[m, pair]
            cut = [(slice(64 * i, 64 * i + 64), slice(128 * i, 128 * i + 128)) for i in range(2)]
            live["gq", pair] = jnp.concatenate([dg(kt[i], ds[:, c]) for i, c in cut], axis=0)
            live["gk", pair] = dg(ds, block_diagonal_rows(qs.T)).T

    def norms_pull(quad):
        for pair in (2 * quad, 2 * quad + 1):
            qs, kt = r.qs[m, pair].astype(F32), r.kt[m, pair].astype(F32)
            gq = head_norm_pull(live["gq", pair] * 0.125, qs * 8.0, r.qi[m, pair])
            gk = head_norm_pull(live["gk", pair], kt, r.ki[m, pair])
            live["gq", pair], live["gk", pair] = gq.astype(BF16), gk.astype(BF16)

    def turn(quad):
        for pair in (2 * quad, 2 * quad + 1):
            for name, start in (("gq", 0), ("gk", 1024)):
                column = start + 128 * pair
                r.gproj[m, :, column : column + 128] = live[name, pair].T

    for stage in (project, probs_pull, scores_pull, values_pull, heads_pull, norms_pull, turn):
        for quad in range(4):
            stage(quad)


def input_pull(m, r):
    gproj = r.gproj[m]
    for j in range(4):
        r.gn[:, 256*j:256*j+256] = dg(gproj, r.wqkv_t[:, 256*j:256*j+256])
    gn = r.gn[...]
    n = r.normed[m].astype(F32)
    first = jnp.mean(gn, axis=-1, keepdims=True)
    second = jnp.mean(gn * n, axis=-1, keepdims=True)
    dx = (gn - first - n * second) * r.xinv[m][:, :1]
    r.gout[m] = (r.gin[m].astype(F32) + dx).astype(BF16)

def transpose_weights(r):
    for j in range(8):
        r.wqkv_t[:, 128*j:128*j+128] = r.wqkv[128*j:128*j+128, :].T
        r.wout_t[:, 128*j:128*j+128] = r.wout[128*j:128*j+128, :].T
    for j in range(6):
        c = slice(512 * j, 512 * j + 512)
        r.columns[:, c] = dg(jnp.ones((16, 1024), BF16), r.wqkv[:, c])


def spread(r, name, column, rows):
    getattr(r, name)[:, :, :, column : column + 128] = rows.T.reshape(16, 2, 32, 128)


def swap(p, mask):
    if mask == 1:
        return p + 1 - 2 * lax.rem(p, 2)
    if mask == 2:
        return lax.rem(p + 2, 4)
    return 3 - p


def relay_kernel(names, *refs):
    r = types.SimpleNamespace(**dict(zip(names, refs)))
    r.xin, r.normed = r.acts.at[0], r.acts.at[1]
    section = lax.axis_index("section")
    last = lax.axis_size("section") - 1
    after = lax.rem(section + 1, last + 1)
    before = lax.rem(section + last, last + 1)
    is_first = section == 0
    is_last = section == last
    place = lax.axis_index("dp")
    core = lax.rem(place, 2)
    z = lax.rem(place // 2, 4)
    y = place // 8
    partner = place + 1 - 2 * core
    y_peers = {a: place + 8 * (swap(y, a) - y) for a in (1, 2, 3)}
    z_peers = {a: place + 2 * (swap(z, a) - z) for a in (1, 2, 3)}
    early = jnp.logical_not(is_first)
    kind = (last - section) // last

    loads = [
        pltpu.make_async_copy(r.w_qkv_hbm.at[0, pl.ds(0, 768)], r.wqkv.at[pl.ds(0, 768)], r.load.at[0]),
        pltpu.make_async_copy(r.w_qkv_hbm.at[0, pl.ds(768, 256)], r.wqkv.at[pl.ds(768, 256)], r.load.at[1]),
        pltpu.make_async_copy(r.w_out_hbm.at[0], r.wout, r.load.at[6]),
    ]

    labels = pltpu.make_async_copy(r.segments_hbm, r.segments, r.load.at[7])

    def entry(m):
        return pltpu.make_async_copy(r.patches.at[m, 0], r.xin.at[m], r.load.at[2 + m])

    def end_gradient(m):
        return pltpu.make_async_copy(r.cotangent.at[m, 0], r.gin.at[m], r.load.at[4 + m])

    def pass_on(m, i):
        c = pl.ds(CHUNKS[i].start, CHUNKS[i].stop - CHUNKS[i].start)
        return pltpu.make_async_remote_copy(
            src_ref=r.xout.at[m, :, c], dst_ref=r.acts.at[0, m, :, c],
            send_sem=r.x_send.at[m, i], recv_sem=r.x_recv.at[m, i],
            device_id={"section": after}, device_id_type=MESH,
        )

    def pass_back(m, i):
        c = pl.ds(CHUNKS[i].start, CHUNKS[i].stop - CHUNKS[i].start)
        return pltpu.make_async_remote_copy(
            src_ref=r.gout.at[m, :, c], dst_ref=r.gin.at[m, :, c],
            send_sem=r.g_send.at[m, i], recv_sem=r.g_recv.at[m, i],
            device_id={"section": before}, device_id_type=MESH,
        )

    def keep_output(m):
        return pltpu.make_async_copy(r.xout.at[m], r.outputs.at[0, m, 0], r.store.at[m])

    def keep_gradient(m):
        return pltpu.make_async_copy(r.gout.at[m], r.input_grads.at[0, m, 0], r.store.at[2 + m])

    def share(name, m, index):
        return pltpu.make_async_remote_copy(
            src_ref=getattr(r, name).at[m], dst_ref=getattr(r, "their_" + name).at[m],
            send_sem=r.share_send.at[index, m], recv_sem=r.share_recv.at[index, m],
            device_id={"dp": partner}, device_id_type=MESH,
        )

    shared = ["normed", "mixed", "gin", "gproj"]

    def axes(half):
        return ((y, y_peers), (z, z_peers)) if half == 0 else ((z, z_peers), (y, y_peers))

    def masks(j):
        return (1, 3) if j % 2 == 0 else (3, 1)

    def block(half, j, position):
        return r.part.at[0, j, position] if half == 0 else r.part.at[1, j, :, position]

    def send(half, j, step):
        (p, p_peers), (q, q_peers) = axes(half)
        a, b = masks(j)
        if step == 0:
            source, target, peer = block(half, j, swap(p, 2)), r.far_in, p_peers[a]
        elif step == 1:
            source, target, peer = block(half, j, swap(p, a)), r.near_in, p_peers[a]
        elif step == 2:
            source, target, peer = r.far_sum.at[half, j], r.last_in, p_peers[b]
        else:
            a = step - 2
            source, target, peer = r.row.at[half, j, swap(q, a)], r.row_in.at[a - 1], q_peers[a]
        return pltpu.make_async_remote_copy(
            src_ref=source, dst_ref=target.at[half, j],
            send_sem=r.sum_send.at[half, j, step], recv_sem=r.sum_recv.at[half, j, step],
            device_id={"dp": peer}, device_id_type=MESH,
        )

    def sum_one(half, j):
        (p, _), _ = axes(half)
        send(half, j, 0).wait_recv()
        held = block(half, j, swap(p, masks(j)[1]))[...].astype(F32)
        r.far_sum[half, j] = (held + r.far_in[half, j].astype(F32)).astype(BF16)
        send(half, j, 2).start()

    def sum_two(half, j):
        (p, _), _ = axes(half)
        send(half, j, 1).wait_recv()
        send(half, j, 2).wait_recv()
        total = block(half, j, p)[...].astype(F32) + r.near_in[half, j].astype(F32)
        r.row[half, j] = (total + r.last_in[half, j].astype(F32)).astype(BF16)
        for step in (3, 4, 5):
            send(half, j, step).start()

    def sum_three(half, j):
        _, (q, _) = axes(half)
        total = r.row[half, j, q].astype(F32)
        for step in (3, 4, 5):
            send(half, j, step).wait_recv()
        for k in range(3):
            total = total + r.row_in[k, half, j].astype(F32)
        column = 2048 * half + 512 * j
        if column < 3072:
            r.total_qkv[0, :, column : column + 512] = total
        else:
            r.total_out_t[:, column - 3072 : column - 2560] = total

    @pl.when(is_first)
    def _():
        for m in range(2):
            entry(m).start()

    labels.start()
    loads[0].start()

    @pl.when(is_last)
    def _():
        for m in range(2):
            end_gradient(m).start()

    barrier = pltpu.get_barrier_semaphore()
    for neighbour in (before, after):
        pl.semaphore_signal(barrier, inc=1, device_id={"section": neighbour}, device_id_type=MESH)
    for peer in [partner, *y_peers.values(), *z_peers.values()]:
        pl.semaphore_signal(barrier, inc=1, device_id={"dp": peer}, device_id_type=MESH)

    @pl.when(early)
    def _():
        for load in loads[1:]:
            load.start()
        for load in loads:
            load.wait()
        transpose_weights(r)

    def forward(m):
        @pl.when(is_first)
        def _():
            entry(m).wait()
            normalise(m, r)

        @pl.when(jnp.logical_not(is_first))
        def _():
            pass_on(m, 0).wait_recv()

        opening = jnp.logical_and(m == 0, jnp.logical_not(early))

        @pl.when(opening)
        def _():
            loads[0].wait()
            for load in loads[1:]:
                load.start()

        project_head(m, kind, r)

        @pl.when(jnp.logical_not(is_first))
        def _():
            pass_on(m, 1).wait_recv()

        @pl.when(opening)
        def _():
            r.columns[...] = jnp.zeros((16, 3072), F32)
            for load in loads[1:]:
                load.wait()

        @pl.when(m == 0)
        def _():
            labels.wait()

        attend(m, kind, r)
        project_out(m, r, HEAD)

        @pl.when(m == 0)
        def _():
            pl.semaphore_wait(barrier, 9)

        @pl.when(jnp.logical_not(is_last))
        def _():
            pass_on(m, 0).start()

        project_out(m, r, TAIL)

        @pl.when(jnp.logical_not(is_last))
        def _():
            pass_on(m, 1).start()

        keep_output(m).start()
        share("normed", m, 0).start()
        share("mixed", m, 1).start()

    def spread_normed():
        for m in range(2):
            share("normed", m, 0).wait_recv()
            share("mixed", m, 1).wait_recv()
        for m in range(2):
            spread(r, "normed_t", 128 * m, r.normed[m])
            spread(r, "normed_t", 256 + 128 * m, r.their_normed[m])

    def backward(m):
        @pl.when(jnp.logical_and(m == 0, jnp.logical_not(early)))
        def _():
            transpose_weights(r)

        @pl.when(jnp.logical_and(m == 0, is_first))
        def _():
            spread_normed()

        @pl.when(is_last)
        def _():
            end_gradient(m).wait()

        @pl.when(jnp.logical_not(is_last))
        def _():
            pass_back(m, 0).wait_recv()

        mixed_pull_head(m, r)

        @pl.when(jnp.logical_not(is_last))
        def _():
            pass_back(m, 1).wait_recv()

        share("gin", m, 2).start()
        attend_pull(m, r)
        share("gproj", m, 3).start()

        @pl.when(jnp.logical_not(is_first))
        def _():
            input_pull(m, r)
            pass_back(m, 0).start()
            pass_back(m, 1).start()
            keep_gradient(m).start()

    turns = section // last

    @pl.loop(0, 4)
    def _(t):
        back = turns * lax.rem(t, 2) + (1 - turns) * (t // 2)
        m = turns * (t // 2) + (1 - turns) * lax.rem(t, 2)

        @pl.when(back == 0)
        def _():
            forward(m)

        @pl.when(back == 1)
        def _():
            backward(m)

    @pl.when(jnp.logical_not(is_first))
    def _():
        spread_normed()

    for m in range(2):
        share("gproj", m, 3).wait_recv()

    def partial(half, j):
        column = 2048 * half + 512 * j
        if column < 3072:
            rows, name, c = r.normed_t, "gproj", slice(column, column + 512)
        else:
            rows, name, c = r.gin_t, "mixed", slice(column - 3072, column - 2560)
        rows = rows[:, core].reshape(512, 512)
        total = dg(rows[:, :256], getattr(r, name)[:, :, c].reshape(256, 512))
        total = total + dg(rows[:, 256:], getattr(r, "their_" + name)[:, :, c].reshape(256, 512))
        r.part[half, j] = total.astype(BF16).reshape(4, 4, 32, 512)

    pieces = [(half, j) for j in range(4) for half in range(2)]
    for half, j in pieces:
        if (half, j) == (1, 2):
            for m in range(2):
                share("gin", m, 2).wait_recv()
                spread(r, "gin_t", 128 * m, r.gin[m])
                spread(r, "gin_t", 256 + 128 * m, r.their_gin[m])
        partial(half, j)
        send(half, j, 0).start()
        send(half, j, 1).start()

    @pl.when(is_first)
    def _():
        @pl.loop(0, 2)
        def _(m):
            input_pull(m, r)
            keep_gradient(m).start()

    stages = (sum_one, sum_two, sum_three)
    lags = (0, 3, 6)
    for step in range(len(pieces) + lags[-1]):
        for lag, stage in zip(lags, stages):
            if 0 <= step - lag < len(pieces):
                stage(*pieces[step - lag])

    for half, j in pieces:
        for step in range(6):
            send(half, j, step).wait_send()
    for index, name in enumerate(shared):
        for m in range(2):
            share(name, m, index).wait_send()

    for m in range(2):
        keep_output(m).wait()
        keep_gradient(m).wait()

        @pl.when(jnp.logical_not(is_last))
        def _():
            pass_on(m, 0).wait_send()
            pass_on(m, 1).wait_send()

        @pl.when(jnp.logical_not(is_first))
        def _():
            pass_back(m, 0).wait_send()
            pass_back(m, 1).wait_send()


def relay(patches, segments, w_qkv, w_out, cotangent):
    inputs = [
        ("patches", patches, pl.ANY),
        ("segments_hbm", segments, pltpu.HBM),
        ("w_qkv_hbm", w_qkv, pl.ANY),
        ("w_out_hbm", w_out, pl.ANY),
        ("cotangent", cotangent, pl.ANY),
    ]
    stacked = (1,) + patches.shape
    results = [
        ("outputs", stacked, BF16, pl.ANY),
        ("input_grads", stacked, BF16, pl.ANY),
        ("total_qkv", (1, 32, 3072), F32, pltpu.VMEM),
        ("total_out_t", (32, 1024), F32, pltpu.VMEM),
    ]
    block = (2, 128, 1024)
    scratch = [
        ("acts", pltpu.VMEM((2,) + block, BF16)),
        ("segments", pltpu.VMEM(segments.shape, jnp.int32)),
        ("begun", pltpu.VMEM((128, 3072), F32)),
        ("columns", pltpu.VMEM((16, 3072), F32)),
        ("gin", pltpu.VMEM(block, BF16)),
        ("xout", pltpu.VMEM(block, BF16)),
        ("gout", pltpu.VMEM(block, BF16)),
        ("mixed", pltpu.VMEM(block, BF16)),
        ("their_normed", pltpu.VMEM(block, BF16)),
        ("their_mixed", pltpu.VMEM(block, BF16)),
        ("their_gin", pltpu.VMEM(block, BF16)),
        ("their_gproj", pltpu.VMEM((2, 128, 3072), BF16)),
        ("normed_t", pltpu.VMEM((16, 2, 32, 512), BF16)),
        ("gin_t", pltpu.VMEM((16, 2, 32, 512), BF16)),
        ("part", pltpu.VMEM((2, 4, 4, 4, 32, 512), BF16)),
        *((name, pltpu.VMEM((2, 4, 4, 32, 512), BF16)) for name in ("far_in", "near_in", "far_sum", "last_in", "row")),
        ("row_in", pltpu.VMEM((3, 2, 4, 32, 512), BF16)),
        ("sum_send", pltpu.SemaphoreType.DMA((2, 4, 6))),
        ("sum_recv", pltpu.SemaphoreType.DMA((2, 4, 6))),
        ("share_send", pltpu.SemaphoreType.DMA((4, 2))),
        ("share_recv", pltpu.SemaphoreType.DMA((4, 2))),
        ("gproj", pltpu.VMEM((2, 128, 3072), BF16)),
        ("gn", pltpu.VMEM((128, 1024), F32)),
        ("wqkv", pltpu.VMEM((1024, 3072), BF16)),
        ("wout", pltpu.VMEM((1024, 1024), BF16)),
        ("wqkv_t", pltpu.VMEM((3072, 1024), BF16)),
        ("wout_t", pltpu.VMEM((1024, 1024), BF16)),
        ("xinv", pltpu.VMEM((2, 128, 128), F32)),
        ("qs", pltpu.VMEM((2, 8, 128, 128), BF16)),
        ("kt", pltpu.VMEM((2, 8, 128, 128), BF16)),
        ("v", pltpu.VMEM((2, 8, 128, 128), BF16)),
        ("qi", pltpu.VMEM((2, 8, 2, 128), F32)),
        ("ki", pltpu.VMEM((2, 8, 2, 128), F32)),
        ("probs", pltpu.VMEM((2, 8, 128, 256), BF16)),
        ("load", pltpu.SemaphoreType.DMA((8,))),
        ("store", pltpu.SemaphoreType.DMA((4,))),
        ("x_send", pltpu.SemaphoreType.DMA((2, 2))),
        ("x_recv", pltpu.SemaphoreType.DMA((2, 2))),
        ("g_send", pltpu.SemaphoreType.DMA((2, 2))),
        ("g_recv", pltpu.SemaphoreType.DMA((2, 2))),
    ]
    names = [i[0] for i in inputs] + [o[0] for o in results] + [s[0] for s in scratch]
    return pl.pallas_call(
        functools.partial(relay_kernel, names),
        out_shape=[jax.ShapeDtypeStruct(o[1], o[2]) for o in results],
        in_specs=[pl.BlockSpec(memory_space=i[2]) for i in inputs],
        out_specs=[pl.BlockSpec(memory_space=o[3]) for o in results],
        scratch_shapes=[s[1] for s in scratch],
        compiler_params=pltpu.CompilerParams(
            collective_id=0, has_side_effects=True, vmem_limit_bytes=58 << 20
        ),
        name="relay",
    )(*[i[1] for i in inputs])


def settle_kernel(count, *refs):
    sources, targets, held = refs[:count], refs[count : 2 * count], refs[2 * count : 3 * count]
    read, written = refs[-2:]
    into = [pltpu.make_async_copy(a, b, read.at[i]) for i, (a, b) in enumerate(zip(sources, held))]
    out = [pltpu.make_async_copy(a, b, written.at[i]) for i, (a, b) in enumerate(zip(held, targets))]
    for copy in into:
        copy.start()
    for first, second in zip(into, out):
        first.wait()
        second.start()
    for copy in out:
        copy.wait()


def settle(arrays):
    return pl.pallas_call(
        functools.partial(settle_kernel, len(arrays)),
        out_shape=[jax.ShapeDtypeStruct(a.shape, a.dtype) for a in arrays],
        in_specs=[pl.BlockSpec(memory_space=pl.ANY)] * len(arrays),
        out_specs=[pl.BlockSpec(memory_space=pl.ANY)] * len(arrays),
        scratch_shapes=[pltpu.VMEM(a.shape, a.dtype) for a in arrays]
        + [pltpu.SemaphoreType.DMA((len(arrays),))] * 2,
        name="settle",
    )(*arrays)


def on_device(patches, segment_ids, weights_qkv, weights_out, cotangent):
    produced, grads, total_qkv, total_out_t = settle(
        relay(patches, segment_ids, weights_qkv, weights_out, cotangent)
    )
    return (produced, grads, total_qkv, total_out_t.T[None])


def solution(mesh):
    return jax.shard_map(
        on_device,
        mesh=mesh,
        in_specs=(
            P(None, "dp", None, None),
            P(None, "dp", None),
            P("section", None, None),
            P("section", None, None),
            P(None, "dp", None, None),
        ),
        out_specs=(
            P("section", None, "dp", None, None),
            P("section", None, "dp", None, None),
            P("section", "dp", None),
            P("section", None, "dp"),
        ),
        check_vma=False,
    )
```
